32 devices in a mesh: section: 2 (over core), dp: 4 (over z), seq: 4 (over y, x).
Axes of the slice: x: 2, y: 2, z: 4, core: 2. Of those that a mesh axis runs over, the one named last changes fastest.
Arguments:
- block_inputs: bfloat16 [2, 16, 768, 800], P('section', 'dp', 'seq'), may hold values from -6 to 6
- cotangent: bfloat16 [16, 768, 800], P('dp', 'seq'), may hold values from -6 to 6
- segment_ids: int32 [16, 768], P('dp', 'seq'), may hold values from 0 to 7, as said below
- in_gain: float32 [2, 800], P('section'), may hold values from 0.5 to 1.5
- in_shift: float32 [2, 800], P('section'), may hold values from -3 to 3
- down_weight: bfloat16 [2, 800, 400], P('section'), may hold values from -0.21875 to 0.21875
- down_bias: float32 [2, 400], P('section'), may hold values from -3 to 3
- mid_gain: float32 [2, 400], P('section'), may hold values from 0.5 to 1.5
- mid_shift: float32 [2, 400], P('section'), may hold values from -3 to 3
- enc_kernel: bfloat16 [5, 400, 400], replicated, may hold values from -0.125 to 0.125
- dec_kernel: bfloat16 [3, 400, 400], replicated, may hold values from -0.1875 to 0.1875
- conv_bias: float32 [2, 400], P('section'), may hold values from -3 to 3
- out_gain: float32 [2, 400], P('section'), may hold values from 0.5 to 1.5
- out_shift: float32 [2, 400], P('section'), may hold values from -3 to 3
- up_weight: bfloat16 [2, 400, 800], P('section'), may hold values from -0.3125 to 0.3125
- up_bias: float32 [2, 800], P('section'), may hold values from -3 to 3
Outputs:
- block_outputs: bfloat16 [2, 16, 768, 800], P('section', 'dp', 'seq')
- input_grads: bfloat16 [2, 16, 768, 800], P('section', 'dp', 'seq')
- in_gain_grad: float32 [2, 800], P('section')
- in_shift_grad: float32 [2, 800], P('section')
- down_weight_grad: float32 [2, 800, 400], P('section')
- down_bias_grad: float32 [2, 400], P('section')
- mid_gain_grad: float32 [2, 400], P('section')
- mid_shift_grad: float32 [2, 400], P('section')
- enc_kernel_grad: float32 [5, 400, 400], P(None, None, 'section')
- dec_kernel_grad: float32 [3, 400, 400], P(None, None, 'section')
- conv_bias_grad: float32 [2, 400], P('section')
- out_gain_grad: float32 [2, 400], P('section')
- out_shift_grad: float32 [2, 400], P('section')
- up_weight_grad: float32 [2, 400, 800], P('section')
- up_bias_grad: float32 [2, 800], P('section')
The draws below stay inside these ranges and needn't reach their ends.
Inputs may be any that keep to these rules, and one draw needn't show every extreme that they name: `segment_ids`: along each row the segment numbers never fall and start at 0; equal numbers mark one sentence pair.
All inputs are finite; a program needn't handle non-finite values.
Results may differ from the reference program's by a relative error of at most 0.0085.
Values may be sent and summed in bfloat16 or wider, within the bound.
A program may use at most 192 MiB of HBM per device.

```python
import jax
import jax.numpy as jnp
from jax import lax

D = 800
H = 400
DILATION = 16
ROWS_DEV = 4
LENGTH = 768
ROWS = 16


top_segment = 7


def draw_segment_ids(key, part):
    key = jax.random.fold_in(key, 11)
    first_key, second_key = jax.random.split(key)
    starts = jax.random.randint(first_key, (ROWS, LENGTH), 0, max(LENGTH // 3, 2))
    starts = (starts == 0).astype(jnp.int32)
    chosen = jax.random.randint(second_key, (ROWS // ROWS_DEV,), 0, ROWS_DEV)
    row_ids = jnp.arange(ROWS)
    chosen_rows = jnp.repeat(chosen, ROWS_DEV)
    busy_row = row_ids % ROWS_DEV == (chosen_rows + 1) % ROWS_DEV
    positions = jnp.arange(LENGTH)
    forced = jnp.zeros((LENGTH,), jnp.int32)
    for step in range(1, 8):
        forced = jnp.where(positions == step * LENGTH // 8, 1, forced)
    starts = jnp.where(busy_row[:, None], jnp.maximum(starts, forced[None, :]), starts)
    starts = starts.at[:, 0].set(0)
    single_doc = row_ids % ROWS_DEV == chosen_rows
    starts = jnp.where(single_doc[:, None], 0, starts)
    return jnp.minimum(jnp.cumsum(starts, axis=1), top_segment).astype(jnp.int32)


def level_of(stream_key, shape, pieces, low, largest):
    level, own = 1.0, jax.random.fold_in(stream_key, 6)
    for axis_at, parts in pieces:
        heights = jnp.exp(jax.random.uniform(jax.random.fold_in(own, axis_at), (parts,), jnp.float32, low / len(pieces), largest / len(pieces)))
        level = level * jnp.repeat(heights, shape[axis_at] // parts).reshape([-1 if axis == axis_at else 1 for axis in range(len(shape))])
    return level


def scatter_about(key, dims, scale, most, shards=(), kind=jnp.bfloat16):
    factor_of = level_of(key, dims, shards, -0.22, 0.18) if shards else 1.0
    result = jax.random.normal(key, dims, jnp.float32) * scale * factor_of
    return jnp.minimum(jnp.maximum(result, -most), most).astype(kind)


def setup_inputs(seed: int = 0) -> dict:
    arg_keys = jax.random.split(jax.random.key(seed), 17)
    return {
        "block_inputs": scatter_about(arg_keys[0], (2, ROWS, LENGTH, D), 1.0, 6.0, ((0, 2), (1, 4), (2, 4))),
        "cotangent": scatter_about(arg_keys[1], (ROWS, LENGTH, D), 1.0, 6.0, ((0, 4), (1, 4))),
        "segment_ids": draw_segment_ids(jax.random.fold_in(arg_keys[16], 71), 0),
        "in_gain": jnp.clip(1.0 + 0.1 * jax.random.normal(arg_keys[3], (2, D), jnp.float32), 0.5, 1.5),
        "in_shift": scatter_about(arg_keys[4], (2, D), 0.5, 3.0, ((0, 2),), jnp.float32),
        "down_weight": scatter_about(arg_keys[5], (2, D, H), D ** -0.5, 0.21875, ((0, 2),)),
        "down_bias": scatter_about(arg_keys[6], (2, H), 0.5, 3.0, ((0, 2),), jnp.float32),
        "mid_gain": jnp.clip(1.0 + 0.1 * jax.random.normal(arg_keys[7], (2, H), jnp.float32), 0.5, 1.5),
        "mid_shift": scatter_about(arg_keys[8], (2, H), 0.5, 3.0, ((0, 2),), jnp.float32),
        "enc_kernel": scatter_about(arg_keys[9], (5, H, H), (5 * H) ** -0.5, 0.125),
        "dec_kernel": scatter_about(arg_keys[10], (3, H, H), (3 * H) ** -0.5, 0.1875),
        "conv_bias": scatter_about(arg_keys[11], (2, H), 0.5, 3.0, ((0, 2),), jnp.float32),
        "out_gain": jnp.clip(1.0 + 0.1 * jax.random.normal(arg_keys[12], (2, H), jnp.float32), 0.5, 1.5),
        "out_shift": scatter_about(arg_keys[13], (2, H), 0.5, 3.0, ((0, 2),), jnp.float32),
        "up_weight": scatter_about(arg_keys[14], (2, H, D), H ** -0.5, 0.3125, ((0, 2),)),
        "up_bias": scatter_about(arg_keys[15], (2, D), 0.5, 3.0, ((0, 2),), jnp.float32),
    }


@jax.custom_vjp
def low(v):
    return lax.optimization_barrier(v.astype(jnp.bfloat16)).astype(jnp.float32)

@jax.custom_vjp
def low_back(v):
    return v

def low_keep(v):
    return (low(v), None)

def low_pass(kept, grad):
    return (grad,)

def back_keep(v):
    return (v, None)

def back_low(kept, grad):
    return (low(grad),)
low.defvjp(low_keep, low_pass)
low_back.defvjp(back_keep, back_low)
epsilon = 1e-05
precise = lax.Precision.HIGHEST

def normalize(values, gain, shift):
    average = lax.optimization_barrier(jnp.mean(values, axis=-1, keepdims=True))
    centred = values - average
    variance = lax.optimization_barrier(jnp.mean(centred * centred, axis=-1, keepdims=True))
    return centred * lax.rsqrt(variance + epsilon) * gain + shift

def shifted_taps(acts, segments, kernel):
    margin = 2 * DILATION
    length = acts.shape[1]
    extended = jnp.pad(acts, ((0, 0), (margin, margin), (0, 0)))
    seg_ext = jnp.pad(segments, ((0, 0), (margin, margin)), constant_values=-1)
    summed = jnp.zeros(acts.shape[:2] + (kernel.shape[2],), jnp.float32)
    for tap in range(kernel.shape[0]):
        offset = (tap - 2) * DILATION
        piece = extended[:, margin + offset:margin + offset + length]
        same_doc = (seg_ext[:, margin + offset:margin + offset + length] == segments).astype(acts.dtype)
        piece = piece * same_doc[..., None]
        summed = summed + jnp.einsum('rth,hg->rtg', piece, kernel[tap], precision=precise)
    return summed

def block(values, segments, params, kernel):
    in_gain, in_shift, down_weight, down_bias, mid_gain, mid_shift, conv_bias, out_gain, out_shift, up_weight, up_bias = params
    first_act = low(jax.nn.gelu(normalize(values, in_gain, in_shift)))
    hidden = low_back(jnp.einsum('rtd,dh->rth', first_act, down_weight, precision=precise)) + down_bias
    mid_act = low(jax.nn.gelu(normalize(hidden, mid_gain, mid_shift)))
    conv_out = low_back(shifted_taps(mid_act, segments, kernel)) + conv_bias
    last_act = low(jax.nn.gelu(normalize(conv_out, out_gain, out_shift)))
    return values + low_back(jnp.einsum('rth,hd->rtd', last_act, up_weight, precision=precise)) + up_bias

def reference(block_inputs, cotangent, segment_ids, in_gain, in_shift, down_weight, down_bias, mid_gain, mid_shift, enc_kernel, dec_kernel, conv_bias, out_gain, out_shift, up_weight, up_bias):
    stacked = tuple((arr.astype(jnp.float32) for arr in (in_gain, in_shift, down_weight, down_bias, mid_gain, mid_shift, conv_bias, out_gain, out_shift, up_weight, up_bias)))
    kernels = (enc_kernel.astype(jnp.float32), dec_kernel.astype(jnp.float32))
    inputs = block_inputs.astype(jnp.float32)
    rows_group = 4
    seg_groups = segment_ids.reshape(ROWS // rows_group, rows_group, LENGTH)

    def run(stacked, kernels, inputs):
        enc_params = tuple((arr[0] for arr in stacked))
        dec_params = tuple((arr[1] for arr in stacked))
        source = inputs[0].reshape(ROWS // rows_group, rows_group, LENGTH, D)
        target = inputs[1].reshape(ROWS // rows_group, rows_group, LENGTH, D)

        def row_step(carry, items):
            src_rows, tgt_rows, seg_rows = items
            encoded = block(src_rows, seg_rows, enc_params, kernels[0])
            passed = low(encoded)
            decoded = block(low_back(passed) + tgt_rows, seg_rows, dec_params, kernels[1])
            return (carry, (passed, decoded))
        start = jnp.zeros((), jnp.float32)
        _, (passed, decoded) = lax.scan(jax.checkpoint(row_step), start, (source, target, seg_groups))
        return (passed.reshape(ROWS, LENGTH, D), decoded.reshape(ROWS, LENGTH, D))
    (passed, decoded), pull = jax.vjp(run, stacked, kernels, inputs)
    grad_stacked, grad_kernels, grad_inputs = pull((jnp.zeros_like(passed), cotangent.astype(jnp.float32)))
    block_outputs = jnp.stack([passed, decoded]).astype(jnp.bfloat16)
    input_grads = grad_inputs.astype(jnp.bfloat16)
    return (block_outputs, input_grads, grad_stacked[0], grad_stacked[1], grad_stacked[2], grad_stacked[3], grad_stacked[4], grad_stacked[5], grad_kernels[0], grad_kernels[1], grad_stacked[6], grad_stacked[7], grad_stacked[8], grad_stacked[9], grad_stacked[10])
```

```python
import functools

import jax
import jax.numpy as jnp
from jax import lax
from jax.experimental import pallas as pl
from jax.experimental.pallas import tpu as pltpu
from jax.sharding import PartitionSpec as P

DILATION = 16
MARGIN = 2 * DILATION
EPSILON = 1e-05
MESH = pl.DeviceIdType.MESH
BF16 = jnp.bfloat16
F32 = jnp.float32
OFFSETS = (-2 * DILATION, -DILATION, DILATION, 2 * DILATION)
ROOT = 0.7978845608028654
CUBIC = 0.044715 * ROOT
VMEM_LIMIT = 60 * 2**20


def dot(left, right, left_dim, right_dim):
    return lax.dot_general(
        left, right, (((left_dim,), (right_dim,)), ((), ())), preferred_element_type=F32
    )


def across(column, width):
    whole, rest = divmod(width, 128)
    pieces = [column] * whole
    if rest:
        pieces.append(column[:, :rest])
    return jnp.concatenate(pieces, axis=1) if len(pieces) > 1 else pieces[0]


def norm_act(values, gain, shift):
    scale = 1.0 / values.shape[-1]
    centred = values - jnp.sum(values, axis=-1, keepdims=True) * scale
    variance = jnp.sum(centred * centred, axis=-1, keepdims=True) * scale
    factor = lax.rsqrt(variance + EPSILON)
    normed = centred * factor
    pre = normed * gain + shift
    square = pre * pre
    half = 0.5 + 0.5 * jnp.tanh(pre * (ROOT + CUBIC * square))
    act = pre * half
    slope = half + act * (1.0 - half) * (2.0 * ROOT + 6.0 * CUBIC * square)
    return normed, factor, act, slope


def norm_act_back(upstream, slope, normed, factor, gain):
    scale = 1.0 / normed.shape[-1]
    at_pre = upstream * slope
    shift_grad = jnp.sum(at_pre, axis=0, keepdims=True)
    gain_grad = jnp.sum(at_pre * normed, axis=0, keepdims=True)
    scaled = at_pre * gain
    first = jnp.sum(scaled, axis=-1, keepdims=True) * scale
    second = jnp.sum(scaled * normed, axis=-1, keepdims=True) * scale
    return factor * (scaled - first - normed * second), gain_grad, shift_grad


def row_block(rows):
    best = 16
    for size in range(16, 257, 16):
        if rows % size == 0:
            best = size
    return best


class Plan:
    def __init__(self, mesh, rows, length, width, inner, enc_taps, dec_taps):
        self.rows, self.length, self.width, self.inner = rows, length, width, inner
        self.half = rows // 2
        self.tokens = self.half * length
        self.taps = (enc_taps, dec_taps)
        self.n_dp, self.n_seq = mesh.shape["dp"], mesh.shape["seq"]
        self.ext = length + 2 * MARGIN
        self.up_main, self.up_rest = divmod(width, 128)
        self.in_main, self.in_rest = divmod(inner, 128)
        lanes = lambda size: -(-size // 128)
        self.in_tiles, self.width_tiles = lanes(inner), lanes(width)
        self.up_rows = self.up_main * inner + self.up_rest * self.in_tiles
        self.down_rows = self.in_main * width + self.in_rest * self.width_tiles
        self.tap_rows = self.in_main * inner + self.in_rest * self.in_tiles
        position = 0
        self.at = {}
        ready = []
        parts = (
            (("up", 1, self.up_rows),),
            (("kernel", 1, self.tap_rows * dec_taps),),
            (("down", 1, self.down_rows), ("up", 0, self.up_rows)),
            (("kernel", 0, self.tap_rows * enc_taps),),
            (("down", 0, self.down_rows),),
        )
        for group in parts:
            for name, block, size in group:
                self.at[name, block] = position
                position += size
            ready.append(position)
        stages = [("section", (1, 1), 2)]
        bits = self.n_seq.bit_length() - 1
        assert self.n_seq == 1 << bits
        for bit in range(bits):
            stages.append(("seq", (1 << bit, 1 << (bits - 1 - bit)), 2))
        left, stride = self.n_dp, 1
        while left > 1:
            radix = 4 if left % 4 == 0 else 2
            assert left % radix == 0
            stages.append(("dp", (stride, stride), radix))
            left, stride = left // radix, stride * radix
        self.stages = stages
        unit = 16
        for _, _, radix in stages:
            unit *= radix
        edges = [0] + [size // unit * unit for size in ready[:-1]] + [-(-ready[-1] // unit) * unit]
        self.chunks = list(zip(edges[:-1], edges[1:]))
        self.pool_rows = edges[-1]
        self.used_rows = ready[-1]


def main_kernel(plan, *refs):
    (
        blocks_in, cot_in, seg_in, in_gain, in_shift, down_in, down_bias, mid_gain, mid_shift,
        enc_in, dec_in, conv_bias, out_gain, out_shift, up_in, up_bias,
        blocks_out, grads_out, pool_out, vec_out,
        xin, cot, wd, wu, ek, dk, vec, seg_side, masks,
        n1, s1, q1, n2, s2, q2, n3, s3, q3, fa, mid, win, la, outv, cp, hp, gin,
        pool, summed, vsum, vrecv,
        load_sem, pair_send, pair_recv, seg_send, seg_recv, halo_send, halo_recv,
        rs_send, rs_recv, ag_send, ag_recv, vec_send, vec_recv, out_sem, out_send, out_recv,
        *recv_bufs,
    ) = refs
    length, width, inner, half = plan.length, plan.width, plan.inner, plan.half
    kernels = (ek, dk)
    sec = lax.axis_index("section")
    seq = lax.axis_index("seq")
    other = 1 - sec
    other_core = {"section": other}
    right = {"seq": lax.rem(seq + 1, plan.n_seq)}
    left = {"seq": lax.rem(seq + plan.n_seq - 1, plan.n_seq)}
    later_sends = []

    def remote(src, dst, send, recv, device):
        return pltpu.make_async_remote_copy(
            src_ref=src, dst_ref=dst, send_sem=send, recv_sem=recv,
            device_id=device, device_id_type=MESH,
        )

    own_rows = pl.ds(sec * half, half)
    other_rows = pl.ds(other * half, half)
    loads = [
        pltpu.make_async_copy(blocks_in.at[0, own_rows], xin.at[sec], load_sem.at[0]),
        pltpu.make_async_copy(down_in.at[0], wd.at[sec], load_sem.at[1]),
        pltpu.make_async_copy(up_in.at[0], wu.at[sec], load_sem.at[2]),
        pltpu.make_async_copy(enc_in, ek, load_sem.at[3]),
        pltpu.make_async_copy(dec_in, dk, load_sem.at[4]),
        pltpu.make_async_copy(cot_in.at[own_rows], cot, load_sem.at[5]),
    ]
    for load in loads:
        load.start()
    vec[...] = jnp.zeros_like(vec)
    for at, ref in enumerate((in_gain, in_shift, up_bias)):
        vec[sec, at : at + 1, :] = ref[...]
    for at, ref in enumerate((down_bias, mid_gain, mid_shift, conv_bias, out_gain, out_shift)):
        vec[sec, 3 + at : 4 + at, :inner] = ref[...]
    vsum[...] = jnp.zeros_like(vsum)

    digits, peers = [], []
    for axis, strides, radix in plan.stages:
        index = lax.axis_index(axis)
        stride = strides[0] if strides[0] == strides[1] else jnp.where(sec == 0, *strides)
        digit = lax.rem(lax.div(index, stride), radix)
        digits.append(digit)
        peers.append(
            [
                {axis: index + (lax.rem(digit + step, radix) - digit) * stride}
                for step in range(1, radix)
            ]
        )
    greeted = [left, right] + [peer for group in peers for peer in group]
    barrier = pltpu.get_barrier_semaphore()
    for peer in greeted:
        pl.semaphore_signal(barrier, inc=1, device_id=peer, device_id_type=MESH)
    pl.semaphore_wait(barrier, len(greeted))

    pair = [
        remote(blocks_in.at[0, other_rows], xin.at[sec], pair_send.at[0], pair_recv.at[0], other_core),
        remote(vec.at[sec], vec.at[sec], pair_send.at[1], pair_recv.at[1], other_core),
        remote(down_in.at[0], wd.at[sec], pair_send.at[2], pair_recv.at[2], other_core),
        remote(up_in.at[0], wu.at[sec], pair_send.at[3], pair_recv.at[3], other_core),
    ]
    arriving = [
        remote(ref.at[other], ref.at[other], pair_send.at[at], pair_recv.at[at], other_core)
        for at, ref in enumerate((xin, vec, wd, wu))
    ]
    for copy in pair:
        copy.start()
    later_sends.extend(pair)
    seg_copies = [
        remote(seg_in, seg_side.at[0], seg_send.at[0], seg_recv.at[0], right),
        remote(seg_in, seg_side.at[1], seg_send.at[1], seg_recv.at[1], left),
    ]
    for copy in seg_copies:
        copy.start()
    later_sends.extend(seg_copies)

    def wait_block(block):
        @pl.when(sec == block)
        def _():
            for load in loads[:3]:
                load.wait()

        @pl.when(sec != block)
        def _():
            for copy in arriving:
                copy.wait_recv()

    def build_masks():
        for copy in seg_copies:
            copy.wait_recv()
        ext = plan.ext
        place = lax.broadcasted_iota(jnp.int32, (ext, length), 0)
        token = lax.broadcasted_iota(jnp.int32, (ext, length), 1)
        for row in range(half):
            at = pl.ds(sec * half + row, 1)
            own = (seg_in[at, :] + 1).astype(F32)
            before = jnp.where(seq > 0, (seg_side[0, at, :] + 1).astype(F32), 0.0)
            after = jnp.where(seq < plan.n_seq - 1, (seg_side[1, at, :] + 1).astype(F32), 0.0)
            spread = jnp.where(place - MARGIN == token, own, 0.0)
            spread = spread + jnp.where(place + (length - MARGIN) == token, before, 0.0)
            spread = spread + jnp.where(place - (length + MARGIN) == token, after, 0.0)
            numbers = dot(spread.astype(BF16), jnp.ones((length, 128), BF16), 1, 0)
            here = numbers[MARGIN : MARGIN + length]
            for at_offset, offset in enumerate(OFFSETS):
                there = numbers[MARGIN + offset : MARGIN + offset + length]
                masks[at_offset, row] = jnp.where(there == here, 1.0, 0.0).astype(BF16)

    def window(ext_ref, block, row, offset):
        piece = ext_ref[block, row, MARGIN + offset : MARGIN + offset + length, :]
        if offset == 0:
            return piece
        return piece * across(masks[OFFSETS.index(offset), row], inner)

    def params(block):
        wide = [vec[block, at : at + 1, :] for at in range(3)]
        narrow = [vec[block, 3 + at : 4 + at, :inner] for at in range(6)]
        return wide + narrow

    def token_rows(row):
        return pl.ds(pl.multiple_of(row * length, length), length)

    def halo(ref, which, block, row):
        copies = []
        if block == 0 or which == 0:
            copies.append(remote(
                ref.at[block, row, pl.ds(length, MARGIN)], ref.at[block, row, pl.ds(0, MARGIN)],
                halo_send.at[which, block, row, 0], halo_recv.at[which, block, row, 0], right,
            ))
        if block == 0 or which == 1:
            copies.append(remote(
                ref.at[block, row, pl.ds(MARGIN, MARGIN)], ref.at[block, row, pl.ds(length + MARGIN, MARGIN)],
                halo_send.at[which, block, row, 1], halo_recv.at[which, block, row, 1], left,
            ))
        return copies

    def each_row(body):
        def step(row, carry):
            body(row)
            return carry

        lax.fori_loop(0, half, step, 0)

    def entry(block, row):
        values = xin[block, row].astype(F32)
        if block == 1:
            values = values + outv[0, token_rows(row)].astype(F32)
        return values

    def forward_in(block):
        p = params(block)

        def body(row):
            at = token_rows(row)
            normed, factor, act, slope = norm_act(entry(block, row), p[0], p[1])
            n1[block, at] = normed
            s1[block, at] = slope
            q1[block, at] = jnp.broadcast_to(factor, (length, 128))
            act = act.astype(BF16)
            fa[block, at] = act
            hidden = dot(act, wd[block], 1, 0) + p[3]
            normed, factor, act, slope = norm_act(hidden, p[4], p[5])
            n2[block, at] = normed
            s2[block, at] = slope
            q2[block, at] = jnp.broadcast_to(factor, (length, 128))
            mid[block, row, MARGIN : MARGIN + length, :] = act.astype(BF16)
            for copy in halo(mid, 0, block, row):
                copy.start()

        each_row(body)

    def forward_out(block):
        p = params(block)

        def body(row):
            at = token_rows(row)
            for copy in halo(mid, 0, block, row):
                copy.wait()
            total = None
            for tap in range(plan.taps[block]):
                piece = window(mid, block, row, (tap - 2) * DILATION)
                win[block, tap, at] = piece
                term = dot(piece, kernels[block][tap], 1, 0)
                total = term if total is None else total + term
            normed, factor, act, slope = norm_act(total + p[6], p[7], p[8])
            n3[block, at] = normed
            s3[block, at] = slope
            q3[block, at] = jnp.broadcast_to(factor, (length, 128))
            act = act.astype(BF16)
            la[block, at] = act
            result = entry(block, row) + dot(act, wu[block], 1, 0) + p[2]
            outv[block, at] = result.astype(BF16)

        each_row(body)

    def add_wide(block, at, value):
        vsum[block, 0, at : at + 1, :] += value[:, :512]
        vsum[block, 0, at + 1 : at + 2, : width - 512] += value[:, 512:]

    def add_narrow(block, at, value):
        vsum[block, 0, at : at + 1, :inner] += value

    def upstream_of(block, row):
        return cot[row] if block == 1 else gin[1, token_rows(row)]

    def backward_out(block):
        p = params(block)

        def body(row):
            at = token_rows(row)
            incoming = upstream_of(block, row)
            add_wide(block, 4, jnp.sum(incoming.astype(F32), axis=0, keepdims=True))
            d_last = dot(incoming, wu[block], 1, 1)
            d_conv, gain_grad, shift_grad = norm_act_back(
                d_last, s3[block, at], n3[block, at], across(q3[block, at], inner), p[7]
            )
            add_narrow(block, 10, gain_grad)
            add_narrow(block, 11, shift_grad)
            add_narrow(block, 9, jnp.sum(d_conv, axis=0, keepdims=True))
            cp[block, row, MARGIN : MARGIN + length, :] = d_conv.astype(BF16)
            for copy in halo(cp, 1, block, row):
                copy.start()

        each_row(body)

    def backward_in(block):
        p = params(block)

        def body(row):
            at = token_rows(row)
            for copy in halo(cp, 1, block, row):
                copy.wait()
            total = None
            for tap in range(plan.taps[block]):
                piece = window(cp, block, row, -(tap - 2) * DILATION)
                term = dot(piece, kernels[block][tap], 1, 1)
                total = term if total is None else total + term
            d_hidden, gain_grad, shift_grad = norm_act_back(
                total, s2[block, at], n2[block, at], across(q2[block, at], inner), p[4]
            )
            add_narrow(block, 7, gain_grad)
            add_narrow(block, 8, shift_grad)
            add_narrow(block, 6, jnp.sum(d_hidden, axis=0, keepdims=True))
            d_hidden = d_hidden.astype(BF16)
            hp[block, at] = d_hidden
            d_first = dot(d_hidden, wd[block], 1, 1)
            d_entry, gain_grad, shift_grad = norm_act_back(
                d_first, s1[block, at], n1[block, at], across(q1[block, at], width), p[0]
            )
            add_wide(block, 0, gain_grad)
            add_wide(block, 2, shift_grad)
            gin[block, at] = (upstream_of(block, row).astype(F32) + d_entry).astype(BF16)

        each_row(body)

    def to_pool(position, left_value, right_value):
        rows, columns = left_value.shape[1], right_value.shape[1]
        main, rest = divmod(columns, 128)
        product = dot(left_value, right_value[:, : main * 128], 0, 0).astype(BF16)
        for tile in range(main):
            pool[position + tile * rows : position + (tile + 1) * rows, :] = product[
                :, tile * 128 : (tile + 1) * 128
            ]
        position += main * rows
        product = dot(right_value[:, main * 128 :], left_value, 0, 0).astype(BF16)
        for tile in range(-(-rows // 128)):
            lanes = min(128, rows - tile * 128)
            pool[position + tile * rest : position + (tile + 1) * rest, :lanes] = product[
                :, tile * 128 : tile * 128 + lanes
            ]

    def upstream_all(block):
        return jnp.concatenate([upstream_of(block, row) for row in range(half)], axis=0)

    def up_weight_grad(block):
        to_pool(plan.at["up", block], la[block], upstream_all(block))

    def kernel_grad(block):
        grad = jnp.concatenate(
            [cp[block, row, MARGIN : MARGIN + length, :] for row in range(half)], axis=0
        )
        for tap in range(plan.taps[block]):
            to_pool(plan.at["kernel", block] + tap * plan.tap_rows, win[block, tap], grad)

    def down_weight_grad(block):
        to_pool(plan.at["down", block], fa[block], hp[block])

    def shape_of(chunk):
        first, last = plan.chunks[chunk]
        sizes, starts, offsets = [last - first], [first], [first]
        for digit, (_, _, radix) in zip(digits, plan.stages):
            sizes.append(sizes[-1] // radix)
            starts.append(starts[-1] // radix)
            offsets.append(pl.multiple_of(offsets[-1] + digit * sizes[-1], 16))
        return sizes, starts, offsets

    def rs_start(chunk, stage):
        sizes, starts, offsets = shape_of(chunk)
        size, radix = sizes[stage + 1], plan.stages[stage][2]
        for step in range(1, radix):
            part = lax.rem(digits[stage] + step, radix)
            copy = remote(
                pool.at[pl.ds(pl.multiple_of(offsets[stage] + part * size, 16), size)],
                recv_bufs[stage].at[step - 1, pl.ds(starts[stage + 1], size)],
                rs_send.at[chunk, stage, step - 1], rs_recv.at[chunk, stage, step - 1],
                peers[stage][step - 1],
            )
            copy.start()
            later_sends.append(copy)

    def rs_finish(chunk, stage):
        sizes, starts, offsets = shape_of(chunk)
        size, radix = sizes[stage + 1], plan.stages[stage][2]
        for step in range(1, radix):
            slot = recv_bufs[stage].at[step - 1, pl.ds(starts[stage + 1], size)]
            remote(
                slot, slot, rs_send.at[chunk, stage, step - 1], rs_recv.at[chunk, stage, step - 1],
                peers[stage][step - 1],
            ).wait_recv()
        block = row_block(size)
        target = summed if stage + 1 == len(plan.stages) else pool

        def add(at, carry):
            own = pl.ds(pl.multiple_of(offsets[stage + 1] + at * block, 16), block)
            landed = pl.ds(pl.multiple_of(starts[stage + 1] + at * block, 16), block)
            total = pool[own, :].astype(F32)
            for step in range(1, radix):
                total = total + recv_bufs[stage][step - 1, landed, :].astype(F32)
            target[own, :] = total.astype(BF16)
            return carry

        lax.fori_loop(0, size // block, add, 0)

    def ag_start(chunk, stage):
        sizes, starts, offsets = shape_of(chunk)
        part = summed.at[pl.ds(offsets[stage + 1], sizes[stage + 1])]
        for step in range(1, plan.stages[stage][2]):
            copy = remote(
                part, part, ag_send.at[chunk, stage, step - 1], ag_recv.at[chunk, stage, step - 1],
                peers[stage][step - 1],
            )
            copy.start()
            later_sends.append(copy)

    def ag_finish(chunk, stage):
        sizes, starts, offsets = shape_of(chunk)
        size, radix = sizes[stage + 1], plan.stages[stage][2]
        for step in range(1, radix):
            sender = lax.rem(digits[stage] + radix - step, radix)
            part = summed.at[pl.ds(pl.multiple_of(offsets[stage] + sender * size, 16), size)]
            remote(
                part, part, ag_send.at[chunk, stage, step - 1], ag_recv.at[chunk, stage, step - 1],
                peers[stage][step - 1],
            ).wait_recv()

    pool_copies = []

    def pool_done(chunk):
        first, last = plan.chunks[chunk]
        copy = pltpu.make_async_copy(
            summed.at[pl.ds(first, last - first)], pool_out.at[pl.ds(first, last - first)], out_sem.at[chunk]
        )
        copy.start()
        pool_copies.append(copy)

    def chunk_events(chunk):
        if plan.chunks[chunk][0] == plan.chunks[chunk][1]:
            return
        count = len(plan.stages)
        for stage in range(count):
            rs_start(chunk, stage)
            yield
            rs_finish(chunk, stage)
        for stage in reversed(range(count)):
            ag_start(chunk, stage)
            yield
            ag_finish(chunk, stage)
        pool_done(chunk)

    def vector_events(block):
        for stage, (_, _, radix) in enumerate(plan.stages):
            for step in range(1, radix):
                copy = remote(
                    vsum.at[block, stage], vrecv.at[block, stage, step - 1],
                    vec_send.at[block, stage, step - 1], vec_recv.at[block, stage, step - 1],
                    peers[stage][step - 1],
                )
                copy.start()
                later_sends.append(copy)
            yield
            total = vsum[block, stage]
            for step in range(1, radix):
                slot = vrecv.at[block, stage, step - 1]
                remote(
                    slot, slot, vec_send.at[block, stage, step - 1],
                    vec_recv.at[block, stage, step - 1], peers[stage][step - 1],
                ).wait_recv()
                total = total + vrecv[block, stage, step - 1]
            vsum[block, stage + 1] = total

    running = []

    def begin(events):
        if next(events, "done") != "done":
            running.append(events)

    def tick():
        for events in list(running):
            if next(events, "done") == "done":
                running.remove(events)

    wait_block(0)
    build_masks()
    forward_in(0)
    loads[3].wait()
    forward_out(0)
    wait_block(1)
    loads[4].wait()
    loads[5].wait()
    forward_in(1)
    forward_out(1)
    up_weight_grad(1)
    begin(chunk_events(0))
    backward_out(1)
    tick()
    kernel_grad(1)
    begin(chunk_events(1))
    tick()
    backward_in(1)
    tick()
    down_weight_grad(1)
    up_weight_grad(0)
    begin(chunk_events(2))
    begin(vector_events(1))
    tick()
    backward_out(0)
    tick()
    kernel_grad(0)
    begin(chunk_events(3))
    tick()
    backward_in(0)
    tick()
    down_weight_grad(0)
    if plan.pool_rows > plan.used_rows:
        pool[plan.used_rows : plan.pool_rows, :] = jnp.zeros(
            (plan.pool_rows - plan.used_rows, 128), BF16
        )
    begin(chunk_events(4))
    begin(vector_events(0))

    copies = []
    for at, (value, result) in enumerate(((outv, blocks_out), (gin, grads_out))):
        for row in range(half):
            rows = pl.ds(row * length, length)
            target = result.at[0, sec * half + row]
            landing = result.at[0, other * half + row]
            copies.append((
                pltpu.make_async_copy(value.at[sec, rows], target, out_send.at[0, at, row]),
                remote(value.at[other, rows], target, out_send.at[1, at, row], out_recv.at[at, row], other_core),
                remote(value.at[other, rows], landing, out_send.at[1, at, row], out_recv.at[at, row], other_core),
            ))
    for local, away, _ in copies:
        local.start()
        away.start()
    while running:
        tick()
    vec_out[...] = vsum[sec, len(plan.stages)]
    for local, away, arrives in copies:
        local.wait()
        away.wait_send()
        arrives.wait_recv()
    for copy in pool_copies:
        copy.wait()
    for copy in later_sends:
        copy.wait_send()


def final_kernel(plan, blocks_in, grads_in, pool_in, vec, *refs):
    (
        blocks_out, grads_out, g_in_gain, g_in_shift, g_down, g_down_bias, g_mid_gain, g_mid_shift,
        g_enc, g_dec, g_conv_bias, g_out_gain, g_out_shift, g_up, g_up_bias,
        up_pool, down_pool, tap_pool, up_full, down_full, enc_full, dec_full,
        in_sem, out_sem,
    ) = refs
    sec = lax.axis_index("section")
    width, inner = plan.width, plan.inner
    passed = [
        pltpu.make_async_copy(blocks_in, blocks_out, out_sem.at[0]),
        pltpu.make_async_copy(grads_in, grads_out, out_sem.at[1]),
    ]
    for copy in passed:
        copy.start()

    def load(name, target, size, sem):
        start = jnp.where(sec == 0, plan.at[name, 0], plan.at[name, 1])
        copy = pltpu.make_async_copy(pool_in.at[pl.ds(pl.multiple_of(start, 16), size)], target, in_sem.at[sem])
        copy.start()
        return copy

    up_load = load("up", up_pool, plan.up_rows, 0)
    down_load = load("down", down_pool, plan.down_rows, 1)
    tap_loads = []
    at = 0
    for block in (0, 1):
        size = plan.tap_rows * plan.taps[block]
        start = plan.at["kernel", block]
        copy = pltpu.make_async_copy(pool_in.at[pl.ds(start, size)], tap_pool.at[pl.ds(at, size)], in_sem.at[2 + block])
        copy.start()
        tap_loads.append(copy)
        at += size

    def wide(at):
        return jnp.concatenate([vec[at : at + 1, :], vec[at + 1 : at + 2, : width - 512]], axis=1)

    g_in_gain[...] = wide(0)
    g_in_shift[...] = wide(2)
    g_up_bias[...] = wide(4)
    for at, ref in enumerate((g_down_bias, g_mid_gain, g_mid_shift, g_conv_bias, g_out_gain, g_out_shift)):
        ref[...] = vec[6 + at : 7 + at, :inner]

    def rest_of(ref, position, rest, tiles):
        pieces = [ref[position + tile * rest : position + (tile + 1) * rest, :] for tile in range(tiles)]
        return jnp.concatenate(pieces, axis=1).astype(F32)

    def unpack(ref, full, rows, main, rest, tiles):
        for tile in range(main):
            full[:, tile * 128 : (tile + 1) * 128] = ref[tile * rows : (tile + 1) * rows, :].astype(F32)
        left = rest_of(ref, main * rows, rest, tiles)
        full[:, main * 128 :] = left.T[:rows, :]

    up_load.wait()
    unpack(up_pool, up_full, inner, plan.up_main, plan.up_rest, plan.in_tiles)
    up_store = pltpu.make_async_copy(up_full, g_up.at[0], out_sem.at[2])
    up_store.start()
    down_load.wait()
    unpack(down_pool, down_full, width, plan.in_main, plan.in_rest, plan.width_tiles)
    down_store = pltpu.make_async_copy(down_full, g_down.at[0], out_sem.at[3])
    down_store.start()
    part = inner // 2
    row = lax.broadcasted_iota(jnp.int32, (inner, part), 0)
    column = lax.broadcasted_iota(jnp.int32, (inner, part), 1)
    choose = jnp.where(row == column + sec * part, 1.0, 0.0).astype(BF16)
    stores = []
    at = 0
    for block, full, target in ((0, enc_full, g_enc), (1, dec_full, g_dec)):
        tap_loads[block].wait()
        for tap in range(plan.taps[block]):
            main = jnp.concatenate(
                [tap_pool[at + tile * inner : at + (tile + 1) * inner, :] for tile in range(plan.in_main)], axis=1
            )
            lanes = plan.in_main * 128
            rest = rest_of(tap_pool, at + plan.in_main * inner, plan.in_rest, plan.in_tiles)
            rest = rest[:, :inner].astype(BF16)
            full[tap] = dot(main, choose[:lanes], 1, 0) + dot(rest, choose[lanes:], 0, 0)
            at += plan.tap_rows
        copy = pltpu.make_async_copy(full, target, out_sem.at[4 + block])
        copy.start()
        stores.append(copy)
    for copy in passed + [up_store, down_store] + stores:
        copy.wait()


def per_device(plan, *args):
    (
        block_inputs, cotangent, segment_ids, in_gain, in_shift, down_weight, down_bias, mid_gain,
        mid_shift, enc_kernel, dec_kernel, conv_bias, out_gain, out_shift, up_weight, up_bias,
    ) = args
    length, width, inner, half, tokens = plan.length, plan.width, plan.inner, plan.half, plan.tokens
    stages = len(plan.stages)
    most = max(radix for _, _, radix in plan.stages) - 1
    chunks = len(plan.chunks)
    any_spec = pl.BlockSpec(memory_space=pl.ANY)
    vmem_spec = pl.BlockSpec(memory_space=pltpu.VMEM)
    wide = lambda kind: pltpu.VMEM((2, tokens, width), kind)
    narrow = lambda kind: pltpu.VMEM((2, tokens, inner), kind)
    factor = pltpu.VMEM((2, tokens, 128), F32)
    dma = pltpu.SemaphoreType.DMA
    recv_bufs, left = [], plan.pool_rows
    for _, _, radix in plan.stages:
        left //= radix
        recv_bufs.append(pltpu.VMEM((radix - 1, left, 128), BF16))
    enc_taps, dec_taps = plan.taps
    blocks, grads, pool, vectors = pl.pallas_call(
        functools.partial(main_kernel, plan),
        out_shape=(
            jax.ShapeDtypeStruct(block_inputs.shape, BF16),
            jax.ShapeDtypeStruct(block_inputs.shape, BF16),
            jax.ShapeDtypeStruct((plan.pool_rows, 128), BF16),
            jax.ShapeDtypeStruct((16, 512), F32),
        ),
        in_specs=[any_spec, any_spec, vmem_spec, vmem_spec, vmem_spec, any_spec, vmem_spec, vmem_spec,
                  vmem_spec, any_spec, any_spec, vmem_spec, vmem_spec, vmem_spec, any_spec, vmem_spec],
        out_specs=(any_spec, any_spec, any_spec, vmem_spec),
        scratch_shapes=[
            pltpu.VMEM((2, half, length, width), BF16),
            pltpu.VMEM((half, length, width), BF16),
            pltpu.VMEM((2, width, inner), BF16),
            pltpu.VMEM((2, inner, width), BF16),
            pltpu.VMEM((enc_taps, inner, inner), BF16),
            pltpu.VMEM((dec_taps, inner, inner), BF16),
            pltpu.VMEM((2, 16, width), F32),
            pltpu.VMEM((2,) + segment_ids.shape, jnp.int32),
            pltpu.VMEM((len(OFFSETS), half, length, 128), BF16),
            wide(F32), wide(F32), factor,
            narrow(F32), narrow(F32), factor,
            narrow(F32), narrow(F32), factor,
            wide(BF16),
            pltpu.VMEM((2, half, plan.ext, inner), BF16),
            pltpu.VMEM((2, enc_taps, tokens, inner), BF16),
            narrow(BF16),
            wide(BF16),
            pltpu.VMEM((2, half, plan.ext, inner), BF16),
            narrow(BF16),
            wide(BF16),
            pltpu.VMEM((plan.pool_rows, 128), BF16),
            pltpu.VMEM((plan.pool_rows, 128), BF16),
            pltpu.VMEM((2, stages + 1, 16, 512), F32),
            pltpu.VMEM((2, stages, most, 16, 512), F32),
            dma((6,)), dma((4,)), dma((4,)), dma((2,)), dma((2,)),
            dma((2, 2, half, 2)), dma((2, 2, half, 2)),
            dma((chunks, stages, most)), dma((chunks, stages, most)),
            dma((chunks, stages, most)), dma((chunks, stages, most)),
            dma((2, stages, most)), dma((2, stages, most)),
            dma((chunks,)), dma((2, 2, half)), dma((2, half)),
        ] + recv_bufs,
        compiler_params=pltpu.CompilerParams(
            collective_id=0, has_side_effects=True, vmem_limit_bytes=VMEM_LIMIT
        ),
        name="blocks_and_sums",
    )(*args)
    vector = lambda size: jax.ShapeDtypeStruct((1, size), F32)
    part = inner // 2
    return pl.pallas_call(
        functools.partial(final_kernel, plan),
        out_shape=(
            jax.ShapeDtypeStruct(block_inputs.shape, BF16),
            jax.ShapeDtypeStruct(block_inputs.shape, BF16),
            vector(width), vector(width),
            jax.ShapeDtypeStruct((1, width, inner), F32),
            vector(inner), vector(inner), vector(inner),
            jax.ShapeDtypeStruct((enc_taps, inner, part), F32),
            jax.ShapeDtypeStruct((dec_taps, inner, part), F32),
            vector(inner), vector(inner), vector(inner),
            jax.ShapeDtypeStruct((1, inner, width), F32),
            vector(width),
        ),
        in_specs=[any_spec, any_spec, any_spec, vmem_spec],
        out_specs=(any_spec, any_spec, vmem_spec, vmem_spec, any_spec, vmem_spec, vmem_spec, vmem_spec,
                   any_spec, any_spec, vmem_spec, vmem_spec, vmem_spec, any_spec, vmem_spec),
        scratch_shapes=[
            pltpu.VMEM((plan.up_rows, 128), BF16),
            pltpu.VMEM((plan.down_rows, 128), BF16),
            pltpu.VMEM((plan.tap_rows * (enc_taps + dec_taps), 128), BF16),
            pltpu.VMEM((inner, width), F32),
            pltpu.VMEM((width, inner), F32),
            pltpu.VMEM((enc_taps, inner, part), F32),
            pltpu.VMEM((dec_taps, inner, part), F32),
            dma((4,)), dma((6,)),
        ],
        compiler_params=pltpu.CompilerParams(vmem_limit_bytes=VMEM_LIMIT),
        name="unpack_sums",
    )(blocks, grads, pool, vectors)


def solution(mesh):
    def whole(*args):
        rows, length, width = (
            args[0].shape[1] // mesh.shape["dp"], args[0].shape[2] // mesh.shape["seq"], args[0].shape[3]
        )
        inner = args[9].shape[1]
        plan = Plan(mesh, rows, length, width, inner, args[9].shape[0], args[10].shape[0])
        by_section = P("section", None)
        weight = P("section", None, None)
        data = P("section", "dp", "seq", None)
        return jax.shard_map(
            functools.partial(per_device, plan),
            mesh=mesh,
            in_specs=(
                data, P("dp", "seq", None), P("dp", "seq"), by_section, by_section, weight, by_section,
                by_section, by_section, P(), P(), by_section, by_section, by_section, weight, by_section,
            ),
            out_specs=(
                data, data, by_section, by_section, weight, by_section, by_section, by_section,
                P(None, None, "section"), P(None, None, "section"),
                by_section, by_section, by_section, weight, by_section,
            ),
            check_vma=False,
        )(*args)

    return whole
```

```python
import functools

import jax
import jax.numpy as jnp
from jax import lax
from jax.experimental import pallas as pl
from jax.experimental.pallas import tpu as pltpu
from jax.sharding import PartitionSpec as P

DILATION = 16
MARGIN = 2 * DILATION
EPSILON = 1e-05
MESH = pl.DeviceIdType.MESH
BF16 = jnp.bfloat16
F32 = jnp.float32
OFFSETS = (-2 * DILATION, -DILATION, DILATION, 2 * DILATION)
ROOT = 0.7978845608028654
CUBIC = 0.044715 * ROOT
VMEM_LIMIT = 60 * 2**20
VECTORS = -1


def dot(left, right, left_dim, right_dim):
    return lax.dot_general(
        left, right, (((left_dim,), (right_dim,)), ((), ())), preferred_element_type=F32
    )


def across(column, width):
    whole, rest = divmod(width, 128)
    pieces = [column] * whole
    if rest:
        pieces.append(column[:, :rest])
    return jnp.concatenate(pieces, axis=1) if len(pieces) > 1 else pieces[0]


def norm_act(values, gain, shift):
    scale = 1.0 / values.shape[-1]
    centred = values - jnp.sum(values, axis=-1, keepdims=True) * scale
    variance = jnp.sum(centred * centred, axis=-1, keepdims=True) * scale
    factor = lax.rsqrt(variance + EPSILON)
    normed = centred * factor
    pre = normed * gain + shift
    square = pre * pre
    half = 0.5 + 0.5 * jnp.tanh(pre * (ROOT + CUBIC * square))
    act = pre * half
    slope = half + act * (1.0 - half) * (2.0 * ROOT + 6.0 * CUBIC * square)
    return normed, factor, act, slope


def norm_act_back(upstream, slope, normed, factor, gain):
    scale = 1.0 / normed.shape[-1]
    at_pre = upstream * slope
    shift_grad = jnp.sum(at_pre, axis=0, keepdims=True)
    gain_grad = jnp.sum(at_pre * normed, axis=0, keepdims=True)
    scaled = at_pre * gain
    first = jnp.sum(scaled, axis=-1, keepdims=True) * scale
    second = jnp.sum(scaled * normed, axis=-1, keepdims=True) * scale
    return factor * (scaled - first - normed * second), gain_grad, shift_grad


def row_block(rows):
    best = 16
    for size in range(16, 257, 16):
        if rows % size == 0:
            best = size
    return best


CHUNKS = ((('up', 1, 0), 'direct'), (('kernel', 1, 9), 'std'), (('down', 1, 0), 'std'), (('up', 0, 0), 'std'), (('kernel', 0, 2), 'std'), (('kernel', 0, 9), 'std'), (('down', 0, 0), 'direct'))


class Plan:
    def __init__(self, mesh, rows, length, width, inner, enc_taps, dec_taps):
        self.rows, self.length, self.width, self.inner = rows, length, width, inner
        self.half = rows // 2
        self.tokens = self.half * length
        self.taps = (enc_taps, dec_taps)
        self.n_dp, self.n_seq = mesh.shape["dp"], mesh.shape["seq"]
        self.ext = length + 2 * MARGIN
        self.up_main, self.up_rest = divmod(width, 128)
        self.in_main, self.in_rest = divmod(inner, 128)
        lanes = lambda size: -(-size // 128)
        self.in_tiles, self.width_tiles = lanes(inner), lanes(width)
        self.up_rows = self.up_main * inner + self.up_rest * self.in_tiles
        self.down_rows = self.up_rows
        self.tap_rows = self.in_main * inner + self.in_rest * self.in_tiles
        position = 0
        self.at, ends = {}, {}
        for name, block, size, pieces in (
            ("up", 1, self.up_rows, 1), ("kernel", 1, self.tap_rows, dec_taps), ("down", 1, self.down_rows, 1),
            ("up", 0, self.up_rows, 1), ("kernel", 0, self.tap_rows, enc_taps), ("down", 0, self.down_rows, 1),
        ):
            self.at[name, block] = position
            for piece in range(pieces):
                position += size
                ends[name, block, piece] = position
        self.used_rows = position
        section = [("section", (1, 1), 2)]
        bits = self.n_seq.bit_length() - 1
        assert self.n_seq == 1 << bits
        halves = [("seq", (1 << bit, 1 << (bits - 1 - bit)), 2) for bit in range(bits)]
        direct = [("seq", (1, 1), self.n_seq)] if bits else []
        layers, left, stride = [], self.n_dp, 1
        while left > 1:
            radix = 4 if left % 4 == 0 else 2
            assert left % radix == 0
            layers.append(("dp", (stride, stride), radix))
            left, stride = left // radix, stride * radix
        orders = {"std": section + halves + layers, "dp first": section + layers + halves,
                  "direct": section + direct + layers}
        self.vec_stages = orders["direct"]
        unit = 32 * self.n_seq * self.n_dp
        self.chunks, first = [], 0
        for (name, block, piece), order in CHUNKS:
            last = ends[name, block, min(piece, self.taps[block] - 1)]
            last = -(-last // unit) * unit if last == self.used_rows else last // unit * unit
            self.chunks.append((first, last, orders[order]))
            first = last
        self.pool_rows = first
        self.landing, self.recv_rows = [], 0
        for first, last, stages in self.chunks:
            size, places = last - first, []
            for _, _, radix in stages:
                size //= radix
                places.append(self.recv_rows)
                self.recv_rows += size * (radix - 1)
            self.landing.append(places)
        self.sent_rows = self.pool_rows - self.pool_rows // (unit // 16)
        self.most_stages = max(len(stages) for _, _, stages in self.chunks)
        self.vec_copies = sum(radix - 1 for _, _, radix in self.vec_stages)


def main_kernel(plan, *refs):
    (
        blocks_in, cot_in, seg_in, in_gain, in_shift, down_in, down_bias, mid_gain, mid_shift,
        enc_in, dec_in, conv_bias, out_gain, out_shift, up_in, up_bias,
        blocks_out, grads_out, pool_out, vec_out,
        xin, cot, wd, wu, ek, dk, vec, seg_side, masks,
        n1, s1, q1, n2, s2, q2, n3, s3, q3, fa, mid, win, la, outv, cp, hp, gin,
        pool, summed, recv, vsum, vtotal, vrecv,
        load_sem, pair_send, pair_recv, seg_send, seg_recv, halo_send, halo_recv,
        pool_send, rs_recv, ag_recv, vec_send, vec_recv, out_sem, out_send, out_recv,
    ) = refs
    length, width, inner, half = plan.length, plan.width, plan.inner, plan.half
    kernels = (ek, dk)
    sec = lax.axis_index("section")
    seq = lax.axis_index("seq")
    other = 1 - sec
    other_core = {"section": other}
    right = {"seq": lax.rem(seq + 1, plan.n_seq)}
    left = {"seq": lax.rem(seq + plan.n_seq - 1, plan.n_seq)}
    later_sends = []

    def remote(src, dst, send, recv, device):
        return pltpu.make_async_remote_copy(
            src_ref=src, dst_ref=dst, send_sem=send, recv_sem=recv,
            device_id=device, device_id_type=MESH,
        )

    own_rows = pl.ds(sec * half, half)
    other_rows = pl.ds(other * half, half)
    loads = [
        pltpu.make_async_copy(blocks_in.at[0, own_rows], xin.at[sec], load_sem.at[0]),
        pltpu.make_async_copy(down_in.at[0], wd.at[sec], load_sem.at[1]),
        pltpu.make_async_copy(up_in.at[0], wu.at[sec], load_sem.at[2]),
        pltpu.make_async_copy(enc_in, ek, load_sem.at[3]),
        pltpu.make_async_copy(dec_in, dk, load_sem.at[4]),
        pltpu.make_async_copy(cot_in.at[own_rows], cot, load_sem.at[5]),
    ]
    for load in loads:
        load.start()
    vec[...] = jnp.zeros_like(vec)
    for at, ref in enumerate((in_gain, in_shift, up_bias)):
        vec[sec, at : at + 1, :] = ref[...]
    for at, ref in enumerate((down_bias, mid_gain, mid_shift, conv_bias, out_gain, out_shift)):
        vec[sec, 3 + at : 4 + at, :inner] = ref[...]
    vsum[...] = jnp.zeros_like(vsum)

    known = {}

    def place(stage):
        if stage not in known:
            axis, strides, radix = stage
            index = lax.axis_index(axis)
            stride = strides[0] if strides[0] == strides[1] else jnp.where(sec == 0, *strides)
            digit = lax.rem(lax.div(index, stride), radix)
            others = [
                {axis: index + (lax.rem(digit + step, radix) - digit) * stride}
                for step in range(1, radix)
            ]
            known[stage] = digit, others
        return known[stage]

    greeted = [peer for stage in plan.vec_stages for peer in place(stage)[1]]
    barrier = pltpu.get_barrier_semaphore()
    for peer in greeted:
        pl.semaphore_signal(barrier, inc=1, device_id=peer, device_id_type=MESH)
    pl.semaphore_wait(barrier, len(greeted))

    pair = [
        remote(blocks_in.at[0, other_rows], xin.at[sec], pair_send.at[0], pair_recv.at[0], other_core),
        remote(vec.at[sec], vec.at[sec], pair_send.at[1], pair_recv.at[1], other_core),
        remote(down_in.at[0], wd.at[sec], pair_send.at[2], pair_recv.at[2], other_core),
        remote(up_in.at[0], wu.at[sec], pair_send.at[3], pair_recv.at[3], other_core),
    ]
    arriving = [
        remote(ref.at[other], ref.at[other], pair_send.at[at], pair_recv.at[at], other_core)
        for at, ref in enumerate((xin, vec, wd, wu))
    ]
    for copy in pair:
        copy.start()
    later_sends.extend(pair)
    seg_copies = [
        remote(seg_in, seg_side.at[0], seg_send.at[0], seg_recv.at[0], right),
        remote(seg_in, seg_side.at[1], seg_send.at[1], seg_recv.at[1], left),
    ]
    for copy in seg_copies:
        copy.start()
    later_sends.extend(seg_copies)

    def wait_block(block):
        @pl.when(sec == block)
        def _():
            for load in loads[:3]:
                load.wait()

        @pl.when(sec != block)
        def _():
            for copy in arriving:
                copy.wait_recv()

    def build_masks():
        for copy in seg_copies:
            copy.wait_recv()
        ext = plan.ext
        place = lax.broadcasted_iota(jnp.int32, (ext, length), 0)
        token = lax.broadcasted_iota(jnp.int32, (ext, length), 1)
        for row in range(half):
            at = pl.ds(sec * half + row, 1)
            own = (seg_in[at, :] + 1).astype(F32)
            before = jnp.where(seq > 0, (seg_side[0, at, :] + 1).astype(F32), 0.0)
            after = jnp.where(seq < plan.n_seq - 1, (seg_side[1, at, :] + 1).astype(F32), 0.0)
            spread = jnp.where(place - MARGIN == token, own, 0.0)
            spread = spread + jnp.where(place + (length - MARGIN) == token, before, 0.0)
            spread = spread + jnp.where(place - (length + MARGIN) == token, after, 0.0)
            numbers = dot(spread.astype(BF16), jnp.ones((length, 128), BF16), 1, 0)
            here = numbers[MARGIN : MARGIN + length]
            for at_offset, offset in enumerate(OFFSETS):
                there = numbers[MARGIN + offset : MARGIN + offset + length]
                masks[at_offset, row] = jnp.where(there == here, 1.0, 0.0).astype(BF16)

    def window(ext_ref, block, row, offset):
        piece = ext_ref[block, row, MARGIN + offset : MARGIN + offset + length, :]
        if offset == 0:
            return piece
        return piece * across(masks[OFFSETS.index(offset), row], inner)

    def params(block):
        wide = [vec[block, at : at + 1, :] for at in range(3)]
        narrow = [vec[block, 3 + at : 4 + at, :inner] for at in range(6)]
        return wide + narrow

    def token_rows(row):
        return pl.ds(pl.multiple_of(row * length, length), length)

    def halo(ref, which, block, row):
        copies = []
        if block == 0 or which == 0:
            copies.append(remote(
                ref.at[block, row, pl.ds(length, MARGIN)], ref.at[block, row, pl.ds(0, MARGIN)],
                halo_send.at[which, block, row, 0], halo_recv.at[which, block, row, 0], right,
            ))
        if block == 0 or which == 1:
            copies.append(remote(
                ref.at[block, row, pl.ds(MARGIN, MARGIN)], ref.at[block, row, pl.ds(length + MARGIN, MARGIN)],
                halo_send.at[which, block, row, 1], halo_recv.at[which, block, row, 1], left,
            ))
        return copies

    def each_row(body):
        def step(row, carry):
            body(row)
            return carry

        lax.fori_loop(0, half, step, 0)

    def entry(block, row):
        values = xin[block, row].astype(F32)
        if block == 1:
            values = values + outv[0, token_rows(row)].astype(F32)
        return values

    def forward_in(block):
        p = params(block)

        def body(row):
            at = token_rows(row)
            normed, factor, act, slope = norm_act(entry(block, row), p[0], p[1])
            n1[block, at] = normed
            s1[block, at] = slope
            q1[block, at] = jnp.broadcast_to(factor, (length, 128))
            act = act.astype(BF16)
            fa[block, at] = act
            hidden = dot(act, wd[block], 1, 1) + p[3]
            normed, factor, act, slope = norm_act(hidden, p[4], p[5])
            n2[block, at] = normed
            s2[block, at] = slope
            q2[block, at] = jnp.broadcast_to(factor, (length, 128))
            mid[block, row, MARGIN : MARGIN + length, :] = act.astype(BF16)
            for copy in halo(mid, 0, block, row):
                copy.start()

        each_row(body)

    def forward_out(block):
        p = params(block)

        def body(row):
            at = token_rows(row)
            for copy in halo(mid, 0, block, row):
                copy.wait()
            total = None
            for tap in range(plan.taps[block]):
                piece = window(mid, block, row, (tap - 2) * DILATION)
                win[block, tap, at] = piece
                term = dot(piece, kernels[block][tap], 1, 0)
                total = term if total is None else total + term
            normed, factor, act, slope = norm_act(total + p[6], p[7], p[8])
            n3[block, at] = normed
            s3[block, at] = slope
            q3[block, at] = jnp.broadcast_to(factor, (length, 128))
            act = act.astype(BF16)
            la[block, at] = act
            result = entry(block, row) + dot(act, wu[block], 1, 0) + p[2]
            outv[block, at] = result.astype(BF16)

        each_row(body)

    def add_wide(block, at, value):
        vsum[block, at : at + 1, :] += value[:, :512]
        vsum[block, at + 1 : at + 2, : width - 512] += value[:, 512:]

    def add_narrow(block, at, value):
        vsum[block, at : at + 1, :inner] += value

    def upstream_of(block, row):
        return cot[row] if block == 1 else gin[1, token_rows(row)]

    def backward_out(block):
        p = params(block)

        def body(row):
            at = token_rows(row)
            incoming = upstream_of(block, row)
            add_wide(block, 4, jnp.sum(incoming.astype(F32), axis=0, keepdims=True))
            d_last = dot(incoming, wu[block], 1, 1)
            d_conv, gain_grad, shift_grad = norm_act_back(
                d_last, s3[block, at], n3[block, at], across(q3[block, at], inner), p[7]
            )
            add_narrow(block, 10, gain_grad)
            add_narrow(block, 11, shift_grad)
            add_narrow(block, 9, jnp.sum(d_conv, axis=0, keepdims=True))
            cp[block, row, MARGIN : MARGIN + length, :] = d_conv.astype(BF16)
            for copy in halo(cp, 1, block, row):
                copy.start()

        each_row(body)

    def backward_mid(block):
        p = params(block)

        def body(row):
            at = token_rows(row)
            for copy in halo(cp, 1, block, row):
                copy.wait()
            total = None
            for tap in range(plan.taps[block]):
                piece = window(cp, block, row, -(tap - 2) * DILATION)
                term = dot(piece, kernels[block][tap], 1, 1)
                total = term if total is None else total + term
            d_hidden, gain_grad, shift_grad = norm_act_back(
                total, s2[block, at], n2[block, at], across(q2[block, at], inner), p[4]
            )
            add_narrow(block, 7, gain_grad)
            add_narrow(block, 8, shift_grad)
            add_narrow(block, 6, jnp.sum(d_hidden, axis=0, keepdims=True))
            hp[block, at] = d_hidden.astype(BF16)

        each_row(body)

    def backward_in(block):
        p = params(block)

        def body(row):
            at = token_rows(row)
            d_first = dot(hp[block, at], wd[block], 1, 0)
            d_entry, gain_grad, shift_grad = norm_act_back(
                d_first, s1[block, at], n1[block, at], across(q1[block, at], width), p[0]
            )
            add_wide(block, 0, gain_grad)
            add_wide(block, 2, shift_grad)
            gin[block, at] = (upstream_of(block, row).astype(F32) + d_entry).astype(BF16)

        each_row(body)

    def to_pool(position, left_value, right_value):
        rows, columns = left_value.shape[1], right_value.shape[1]
        main, rest = divmod(columns, 128)
        product = dot(left_value, right_value[:, : main * 128], 0, 0).astype(BF16)
        for tile in range(main):
            pool[position + tile * rows : position + (tile + 1) * rows, :] = product[
                :, tile * 128 : (tile + 1) * 128
            ]
        position += main * rows
        product = dot(right_value[:, main * 128 :], left_value, 0, 0).astype(BF16)
        for tile in range(-(-rows // 128)):
            lanes = min(128, rows - tile * 128)
            pool[position + tile * rest : position + (tile + 1) * rest, :lanes] = product[
                :, tile * 128 : tile * 128 + lanes
            ]

    def upstream_all(block):
        return jnp.concatenate([upstream_of(block, row) for row in range(half)], axis=0)

    def up_weight_grad(block):
        to_pool(plan.at["up", block], la[block], upstream_all(block))

    def kernel_grad(block, tap):
        grad = jnp.concatenate(
            [cp[block, row, MARGIN : MARGIN + length, :] for row in range(half)], axis=0
        )
        to_pool(plan.at["kernel", block] + tap * plan.tap_rows, win[block, tap], grad)

    def down_weight_grad(block):
        to_pool(plan.at["down", block], hp[block], fa[block])

    pool_copies, running = [], {}

    def sum_chunk(chunk):
        first, last, stages = plan.chunks[chunk]
        places = [place(stage) for stage in stages]
        sizes, offsets = [last - first], [first]
        for (digit, _), (_, _, radix) in zip(places, stages):
            sizes.append(sizes[-1] // radix)
            offsets.append(pl.multiple_of(offsets[-1] + digit * sizes[-1], 16))

        def part(ref, stage, digit):
            size = sizes[stage + 1]
            return ref.at[pl.ds(pl.multiple_of(offsets[stage] + digit * size, 16), size)]

        for stage, (_, _, radix) in enumerate(stages):
            digit, others = places[stage]
            size, landing = sizes[stage + 1], plan.landing[chunk][stage]
            sem = rs_recv.at[chunk * plan.most_stages + stage]
            for step in range(1, radix):
                remote(
                    part(pool, stage, lax.rem(digit + step, radix)),
                    recv.at[pl.ds(landing + (step - 1) * size, size)],
                    pool_send.at[0], sem, others[step - 1],
                ).start()
            yield
            landed = recv.at[pl.ds(landing, (radix - 1) * size)]
            remote(landed, landed, pool_send.at[0], sem, others[0]).wait_recv()
            target = summed if stage + 1 == len(stages) else pool
            block = row_block(size)

            def add(at, carry):
                own = pl.ds(pl.multiple_of(offsets[stage + 1] + at * block, 16), block)
                total = pool[own, :].astype(F32)
                for step in range(radix - 1):
                    from_row = pl.multiple_of(landing + step * size + at * block, 16)
                    total = total + recv[pl.ds(from_row, block), :].astype(F32)
                target[own, :] = total.astype(BF16)
                return carry

            lax.fori_loop(0, size // block, add, 0)
        for stage in reversed(range(len(stages))):
            radix = stages[stage][2]
            digit, others = places[stage]
            size = sizes[stage + 1]
            sem = ag_recv.at[chunk * plan.most_stages + stage]
            own = part(summed, stage, digit)
            for step in range(1, radix):
                remote(own, own, pool_send.at[1], sem, others[step - 1]).start()
            yield
            arriving = summed.at[pl.ds(first, (radix - 1) * size)]
            remote(arriving, arriving, pool_send.at[1], sem, others[0]).wait_recv()
        whole = pl.ds(first, last - first)
        copy = pltpu.make_async_copy(summed.at[whole], pool_out.at[whole], out_sem.at[chunk])
        copy.start()
        pool_copies.append(copy)

    def sum_vectors():
        total, slot = None, 0
        for at, stage in enumerate(plan.vec_stages):
            digit, others = place(stage)
            count = stage[2] - 1
            for step in range(count):
                source = vsum.at[other] if at == 0 else vtotal.at[at - 1]
                remote(
                    source, vrecv.at[slot + step], vec_send.at[0], vec_recv.at[at], others[step]
                ).start()
            yield
            landed = vrecv.at[pl.ds(slot, count)]
            remote(landed, landed, vec_send.at[0], vec_recv.at[at], others[0]).wait_recv()
            total = vsum[sec] if at == 0 else vtotal[at - 1]
            for step in range(count):
                total = total + vrecv[slot + step]
            vtotal[at] = total
            slot += count

    def tick(which):
        if which not in running:
            running[which] = sum_vectors() if which == VECTORS else sum_chunk(which)
        if running[which] is not None and next(running[which], "done") == "done":
            running[which] = None

    def run(steps):
        for step in steps:
            if isinstance(step, int):
                if step == VECTORS or plan.chunks[step][0] < plan.chunks[step][1]:
                    tick(step)
            else:
                step[0](*step[1:])

    results = []

    def send_result(at):
        value, result = ((outv, blocks_out), (gin, grads_out))[at]
        for row in range(half):
            rows = pl.ds(row * length, length)
            target = result.at[0, sec * half + row]
            landing = result.at[0, other * half + row]
            local = pltpu.make_async_copy(value.at[sec, rows], target, out_send.at[0, at, row])
            sems = out_send.at[1, at, row], out_recv.at[at, row]
            away = remote(value.at[other, rows], target, *sems, other_core)
            local.start()
            away.start()
            results.append((local, away, remote(value.at[other, rows], landing, *sems, other_core)))

    wait_block(0)
    build_masks()
    forward_in(0)
    loads[3].wait()
    forward_out(0)
    wait_block(1)
    loads[4].wait()
    loads[5].wait()
    forward_in(1)
    forward_out(1)
    send_result(0)
    if plan.pool_rows > plan.used_rows:
        pool[plan.used_rows : plan.pool_rows, :] = jnp.zeros(
            (plan.pool_rows - plan.used_rows, 128), BF16
        )
    run((
        (up_weight_grad, 1), (backward_out, 1), 0, (kernel_grad, 1, 1), (kernel_grad, 1, 0), (kernel_grad, 1, 2), 0, 1, (backward_mid, 1), 1, (down_weight_grad, 1), (backward_in, 1), 0, (up_weight_grad, 0), 2, 3, 1, (backward_out, 0), 0, 3, (kernel_grad, 0, 0), (kernel_grad, 0, 1), 2, 1, (kernel_grad, 0, 3), (kernel_grad, 0, 4), (kernel_grad, 0, 2), 5, 0, 3, (backward_mid, 0), 4, 5, 1, 2, 4, 3, 2, 5, (down_weight_grad, 0), 0, 1, 6, 3, 4, 5, 6, 2, 4, 1, 5, 2, 3, 6, 1, 0, 4, 5, 2, 6, 3, 1, 5, 4, 2, 6, (backward_in, 0), (send_result, 1), VECTORS, 4, 5, 5, 2, 3, 6, 4, 6, 3, 4,
    ))

    while any(events is not None for events in running.values()):
        run(tuple(range(len(plan.chunks))) + (VECTORS,))
    vec_out[...] = vtotal[len(plan.vec_stages) - 1]
    for local, away, arrives in results:
        local.wait()
        away.wait_send()
        arrives.wait_recv()
    for copy in pool_copies:
        copy.wait()
    for copy in later_sends:
        copy.wait_send()
    for at in range(2):
        everything = summed.at[pl.ds(0, plan.sent_rows)]
        remote(everything, everything, pool_send.at[at], rs_recv.at[0], other_core).wait_send()
    remote(vrecv, vrecv, vec_send.at[0], vec_recv.at[0], other_core).wait_send()


def final_kernel(plan, blocks_in, grads_in, pool_in, vec, *refs):
    (
        blocks_out, grads_out, g_in_gain, g_in_shift, g_down, g_down_bias, g_mid_gain, g_mid_shift,
        g_enc, g_dec, g_conv_bias, g_out_gain, g_out_shift, g_up, g_up_bias,
        bounce, up_pool, down_pool, tap_pool, up_full, down_full, enc_full, dec_full,
        in_sem, out_sem,
    ) = refs
    sec = lax.axis_index("section")
    width, inner = plan.width, plan.inner
    entering = [
        pltpu.make_async_copy(blocks_in, bounce.at[0], in_sem.at[4]),
        pltpu.make_async_copy(grads_in, bounce.at[1], in_sem.at[5]),
    ]
    passed = [
        pltpu.make_async_copy(bounce.at[0], blocks_out, out_sem.at[0]),
        pltpu.make_async_copy(bounce.at[1], grads_out, out_sem.at[1]),
    ]
    for copy in entering:
        copy.start()

    def load(name, target, size, sem):
        start = jnp.where(sec == 0, plan.at[name, 0], plan.at[name, 1])
        copy = pltpu.make_async_copy(pool_in.at[pl.ds(pl.multiple_of(start, 16), size)], target, in_sem.at[sem])
        copy.start()
        return copy

    up_load = load("up", up_pool, plan.up_rows, 0)
    down_load = load("down", down_pool, plan.down_rows, 1)
    tap_loads = []
    at = 0
    for block in (0, 1):
        size = plan.tap_rows * plan.taps[block]
        start = plan.at["kernel", block]
        copy = pltpu.make_async_copy(pool_in.at[pl.ds(start, size)], tap_pool.at[pl.ds(at, size)], in_sem.at[2 + block])
        copy.start()
        tap_loads.append(copy)
        at += size

    def wide(at):
        return jnp.concatenate([vec[at : at + 1, :], vec[at + 1 : at + 2, : width - 512]], axis=1)

    g_in_gain[...] = wide(0)
    g_in_shift[...] = wide(2)
    g_up_bias[...] = wide(4)
    for at, ref in enumerate((g_down_bias, g_mid_gain, g_mid_shift, g_conv_bias, g_out_gain, g_out_shift)):
        ref[...] = vec[6 + at : 7 + at, :inner]

    def rest_of(ref, position, rest, tiles):
        pieces = [ref[position + tile * rest : position + (tile + 1) * rest, :] for tile in range(tiles)]
        return jnp.concatenate(pieces, axis=1).astype(F32)

    def unpack(ref, full, rows, main, rest, tiles):
        for tile in range(main):
            full[:, tile * 128 : (tile + 1) * 128] = ref[tile * rows : (tile + 1) * rows, :].astype(F32)
        left = rest_of(ref, main * rows, rest, tiles)
        full[:, main * 128 :] = left.T[:rows, :]

    for first, second in zip(entering, passed):
        first.wait()
        second.start()
    up_load.wait()
    unpack(up_pool, up_full, inner, plan.up_main, plan.up_rest, plan.in_tiles)
    up_store = pltpu.make_async_copy(up_full, g_up.at[0], out_sem.at[2])
    up_store.start()
    down_load.wait()
    unpack(down_pool, down_full, inner, plan.up_main, plan.up_rest, plan.in_tiles)
    down_store = pltpu.make_async_copy(down_full, g_down.at[0], out_sem.at[3])
    down_store.start()
    part = inner // 2
    row = lax.broadcasted_iota(jnp.int32, (inner, part), 0)
    column = lax.broadcasted_iota(jnp.int32, (inner, part), 1)
    choose = jnp.where(row == column + sec * part, 1.0, 0.0).astype(BF16)
    stores = []
    at = 0
    for block, full, target in ((0, enc_full, g_enc), (1, dec_full, g_dec)):
        tap_loads[block].wait()
        for tap in range(plan.taps[block]):
            main = jnp.concatenate(
                [tap_pool[at + tile * inner : at + (tile + 1) * inner, :] for tile in range(plan.in_main)], axis=1
            )
            lanes = plan.in_main * 128
            rest = rest_of(tap_pool, at + plan.in_main * inner, plan.in_rest, plan.in_tiles)
            rest = rest[:, :inner].astype(BF16)
            full[tap] = dot(main, choose[:lanes], 1, 0) + dot(rest, choose[lanes:], 0, 0)
            at += plan.tap_rows
        copy = pltpu.make_async_copy(full, target, out_sem.at[4 + block])
        copy.start()
        stores.append(copy)
    for copy in passed + [up_store, down_store] + stores:
        copy.wait()


def per_device(plan, *args):
    (
        block_inputs, cotangent, segment_ids, in_gain, in_shift, down_weight, down_bias, mid_gain,
        mid_shift, enc_kernel, dec_kernel, conv_bias, out_gain, out_shift, up_weight, up_bias,
    ) = args
    args = args[:5] + (jnp.swapaxes(down_weight, 1, 2),) + args[6:]
    length, width, inner, half, tokens = plan.length, plan.width, plan.inner, plan.half, plan.tokens
    chunks = len(plan.chunks)
    any_spec = pl.BlockSpec(memory_space=pl.ANY)
    vmem_spec = pl.BlockSpec(memory_space=pltpu.VMEM)
    wide = lambda kind: pltpu.VMEM((2, tokens, width), kind)
    narrow = lambda kind: pltpu.VMEM((2, tokens, inner), kind)
    factor = pltpu.VMEM((2, tokens, 128), F32)
    dma = pltpu.SemaphoreType.DMA
    enc_taps, dec_taps = plan.taps
    blocks, grads, pool, vectors = pl.pallas_call(
        functools.partial(main_kernel, plan),
        out_shape=(
            jax.ShapeDtypeStruct(block_inputs.shape, BF16),
            jax.ShapeDtypeStruct(block_inputs.shape, BF16),
            jax.ShapeDtypeStruct((plan.pool_rows, 128), BF16),
            jax.ShapeDtypeStruct((16, 512), F32),
        ),
        in_specs=[any_spec, any_spec, vmem_spec, vmem_spec, vmem_spec, any_spec, vmem_spec, vmem_spec,
                  vmem_spec, any_spec, any_spec, vmem_spec, vmem_spec, vmem_spec, any_spec, vmem_spec],
        out_specs=(any_spec, any_spec, any_spec, vmem_spec),
        scratch_shapes=[
            pltpu.VMEM((2, half, length, width), BF16),
            pltpu.VMEM((half, length, width), BF16),
            pltpu.VMEM((2, inner, width), BF16),
            pltpu.VMEM((2, inner, width), BF16),
            pltpu.VMEM((enc_taps, inner, inner), BF16),
            pltpu.VMEM((dec_taps, inner, inner), BF16),
            pltpu.VMEM((2, 16, width), F32),
            pltpu.VMEM((2,) + segment_ids.shape, jnp.int32),
            pltpu.VMEM((len(OFFSETS), half, length, 128), BF16),
            wide(F32), wide(F32), factor,
            narrow(F32), narrow(F32), factor,
            narrow(F32), narrow(F32), factor,
            wide(BF16),
            pltpu.VMEM((2, half, plan.ext, inner), BF16),
            pltpu.VMEM((2, enc_taps, tokens, inner), BF16),
            narrow(BF16),
            wide(BF16),
            pltpu.VMEM((2, half, plan.ext, inner), BF16),
            narrow(BF16),
            wide(BF16),
            pltpu.VMEM((plan.pool_rows, 128), BF16),
            pltpu.VMEM((plan.pool_rows, 128), BF16),
            pltpu.VMEM((plan.recv_rows, 128), BF16),
            pltpu.VMEM((2, 16, 512), F32),
            pltpu.VMEM((len(plan.vec_stages), 16, 512), F32),
            pltpu.VMEM((plan.vec_copies, 16, 512), F32),
            dma((6,)), dma((4,)), dma((4,)), dma((2,)), dma((2,)),
            dma((2, 2, half, 2)), dma((2, 2, half, 2)),
            dma((2,)), dma((chunks * plan.most_stages,)), dma((chunks * plan.most_stages,)),
            dma((1,)), dma((len(plan.vec_stages),)),
            dma((chunks,)), dma((2, 2, half)), dma((2, half)),
        ],
        compiler_params=pltpu.CompilerParams(
            collective_id=0, has_side_effects=True, vmem_limit_bytes=VMEM_LIMIT
        ),
        name="blocks_and_sums",
    )(*args)
    vector = lambda size: jax.ShapeDtypeStruct((1, size), F32)
    part = inner // 2
    results = pl.pallas_call(
        functools.partial(final_kernel, plan),
        out_shape=(
            jax.ShapeDtypeStruct(block_inputs.shape, BF16),
            jax.ShapeDtypeStruct(block_inputs.shape, BF16),
            vector(width), vector(width),
            jax.ShapeDtypeStruct((1, inner, width), F32),
            vector(inner), vector(inner), vector(inner),
            jax.ShapeDtypeStruct((enc_taps, inner, part), F32),
            jax.ShapeDtypeStruct((dec_taps, inner, part), F32),
            vector(inner), vector(inner), vector(inner),
            jax.ShapeDtypeStruct((1, inner, width), F32),
            vector(width),
        ),
        in_specs=[any_spec, any_spec, any_spec, vmem_spec],
        out_specs=(any_spec, any_spec, vmem_spec, vmem_spec, any_spec, vmem_spec, vmem_spec, vmem_spec,
                   any_spec, any_spec, vmem_spec, vmem_spec, vmem_spec, any_spec, vmem_spec),
        scratch_shapes=[
            pltpu.VMEM((2,) + block_inputs.shape, BF16),
            pltpu.VMEM((plan.up_rows, 128), BF16),
            pltpu.VMEM((plan.down_rows, 128), BF16),
            pltpu.VMEM((plan.tap_rows * (enc_taps + dec_taps), 128), BF16),
            pltpu.VMEM((inner, width), F32),
            pltpu.VMEM((inner, width), F32),
            pltpu.VMEM((enc_taps, inner, part), F32),
            pltpu.VMEM((dec_taps, inner, part), F32),
            dma((6,)), dma((6,)),
        ],
        compiler_params=pltpu.CompilerParams(vmem_limit_bytes=VMEM_LIMIT),
        name="unpack_sums",
    )(blocks, grads, pool, vectors)
    return results[:4] + (jnp.swapaxes(results[4], 1, 2),) + results[5:]


def solution(mesh):
    def whole(*args):
        rows, length, width = (
            args[0].shape[1] // mesh.shape["dp"], args[0].shape[2] // mesh.shape["seq"], args[0].shape[3]
        )
        inner = args[9].shape[1]
        plan = Plan(mesh, rows, length, width, inner, args[9].shape[0], args[10].shape[0])
        by_section = P("section", None)
        weight = P("section", None, None)
        data = P("section", "dp", "seq", None)
        return jax.shard_map(
            functools.partial(per_device, plan),
            mesh=mesh,
            in_specs=(
                data, P("dp", "seq", None), P("dp", "seq"), by_section, by_section, weight, by_section,
                by_section, by_section, P(), P(), by_section, by_section, by_section, weight, by_section,
            ),
            out_specs=(
                data, data, by_section, by_section, weight, by_section, by_section, by_section,
                P(None, None, "section"), P(None, None, "section"),
                by_section, by_section, by_section, weight, by_section,
            ),
            check_vma=False,
        )(*args)

    return whole
```

```python
import functools

import jax
import jax.numpy as jnp
from jax import lax
from jax.experimental import pallas as pl
from jax.experimental.pallas import tpu as pltpu
from jax.sharding import PartitionSpec as P

DILATION = 16
MARGIN = 2 * DILATION
EPSILON = 1e-05
MESH = pl.DeviceIdType.MESH
BF16 = jnp.bfloat16
F32 = jnp.float32
OFFSETS = (-2 * DILATION, -DILATION, DILATION, 2 * DILATION)
ROOT = 0.7978845608028654
CUBIC = 0.044715 * ROOT
VMEM_LIMIT = 60 * 2**20
VECTORS = -1


def dot(left, right, left_dim, right_dim):
    return lax.dot_general(
        left, right, (((left_dim,), (right_dim,)), ((), ())), preferred_element_type=F32
    )


def across(column, width):
    whole, rest = divmod(width, 128)
    pieces = [column] * whole
    if rest:
        pieces.append(column[:, :rest])
    return jnp.concatenate(pieces, axis=1) if len(pieces) > 1 else pieces[0]


def norm_act(values, gain, shift):
    scale = 1.0 / values.shape[-1]
    centred = values - jnp.sum(values, axis=-1, keepdims=True) * scale
    variance = jnp.sum(centred * centred, axis=-1, keepdims=True) * scale
    factor = lax.rsqrt(variance + EPSILON)
    normed = centred * factor
    pre = normed * gain + shift
    square = pre * pre
    half = 0.5 + 0.5 * jnp.tanh(pre * (ROOT + CUBIC * square))
    act = pre * half
    slope = half + act * (1.0 - half) * (2.0 * ROOT + 6.0 * CUBIC * square)
    return normed, factor, act, slope


def norm_act_back(upstream, slope, normed, factor, gain):
    scale = 1.0 / normed.shape[-1]
    at_pre = upstream * slope
    shift_grad = jnp.sum(at_pre, axis=0, keepdims=True)
    gain_grad = jnp.sum(at_pre * normed, axis=0, keepdims=True)
    scaled = at_pre * gain
    first = jnp.sum(scaled, axis=-1, keepdims=True) * scale
    second = jnp.sum(scaled * normed, axis=-1, keepdims=True) * scale
    return factor * (scaled - first - normed * second), gain_grad, shift_grad


def row_block(rows):
    best = 16
    for size in range(16, 257, 16):
        if rows % size == 0:
            best = size
    return best


PARTS = 40
CHUNKS = ((7, 'std'), (11, 'std'), (17, 'std'), (24, 'std'), (26, 'std'), (32, 'std'), (34, 'std'), (40, 'std'))


class Plan:
    def __init__(self, mesh, rows, length, width, inner, enc_taps, dec_taps):
        self.rows, self.length, self.width, self.inner = rows, length, width, inner
        self.half = rows // 2
        self.tokens = self.half * length
        self.taps = (enc_taps, dec_taps)
        self.n_dp, self.n_seq = mesh.shape["dp"], mesh.shape["seq"]
        self.ext = length + 2 * MARGIN
        self.up_main, self.up_rest = divmod(width, 128)
        self.in_main, self.in_rest = divmod(inner, 128)
        lanes = lambda size: -(-size // 128)
        self.in_tiles, self.width_tiles = lanes(inner), lanes(width)
        self.up_rows = self.up_main * inner + self.up_rest * self.in_tiles
        self.down_rows = self.up_rows
        self.tap_rows = self.in_main * inner + self.in_rest * self.in_tiles
        position = 0
        self.at = {}
        for name, block, size, pieces in (
            ("up", 1, self.up_rows, 1), ("kernel", 1, self.tap_rows, dec_taps), ("down", 1, self.down_rows, 1),
            ("up", 0, self.up_rows, 1), ("kernel", 0, self.tap_rows, enc_taps), ("down", 0, self.down_rows, 1),
        ):
            self.at[name, block] = position
            position += size * pieces
        self.used_rows = position
        section = [("section", (1, 1), 2)]
        bits = self.n_seq.bit_length() - 1
        assert self.n_seq == 1 << bits
        halves = [("seq", (1 << bit, 1 << (bits - 1 - bit)), 2) for bit in range(bits)]
        direct = [("seq", (1, 1), self.n_seq)] if bits else []
        layers, left, stride = [], self.n_dp, 1
        while left > 1:
            radix = 4 if left % 4 == 0 else 2
            assert left % radix == 0
            layers.append(("dp", (stride, stride), radix))
            left, stride = left // radix, stride * radix
        orders = {"std": section + halves + layers, "dp first": section + layers + halves,
                  "direct": section + direct + layers}
        self.vec_stages = orders["direct"]
        unit = 32 * self.n_seq * self.n_dp
        self.pool_rows = -(-self.used_rows // unit) * unit
        nominal = -(-self.used_rows // 512) * 512
        self.chunks, first = [], 0
        for end, order in CHUNKS:
            last = self.pool_rows if end == PARTS else nominal * end // PARTS // unit * unit
            self.chunks.append((first, last, orders[order]))
            first = last
        self.landing, self.recv_rows = [], 0
        for first, last, stages in self.chunks:
            size, places = last - first, []
            for _, _, radix in stages:
                size //= radix
                places.append(self.recv_rows)
                self.recv_rows += size * (radix - 1)
            self.landing.append(places)
        self.sent_rows = self.pool_rows - self.pool_rows // (unit // 16)
        self.most_stages = max(len(stages) for _, _, stages in self.chunks)
        self.vec_copies = sum(radix - 1 for _, _, radix in self.vec_stages)


def main_kernel(plan, *refs):
    (
        blocks_in, cot_in, seg_in, in_gain, in_shift, down_in, down_bias, mid_gain, mid_shift,
        enc_in, dec_in, conv_bias, out_gain, out_shift, up_in, up_bias,
        blocks_out, grads_out, pool_out, vec_out,
        xin, cot, wd, wu, ek, dk, vec, seg_side, masks,
        n1, s1, q1, n2, s2, q2, n3, s3, q3, fa, mid, win, la, outv, cp, hp, gin, dl,
        pool, summed, recv, vsum, vtotal, vrecv,
        load_sem, pair_send, pair_recv, seg_send, seg_recv, halo_send, halo_recv,
        pool_send, rs_recv, ag_recv, vec_send, vec_recv, out_sem, out_send, out_recv,
    ) = refs
    length, width, inner, half = plan.length, plan.width, plan.inner, plan.half
    kernels = (ek, dk)
    sec = lax.axis_index("section")
    seq = lax.axis_index("seq")
    other = 1 - sec
    other_core = {"section": other}
    right = {"seq": lax.rem(seq + 1, plan.n_seq)}
    left = {"seq": lax.rem(seq + plan.n_seq - 1, plan.n_seq)}
    later_sends = []

    def remote(src, dst, send, recv, device):
        return pltpu.make_async_remote_copy(
            src_ref=src, dst_ref=dst, send_sem=send, recv_sem=recv,
            device_id=device, device_id_type=MESH,
        )

    own_rows = pl.ds(sec * half, half)
    other_rows = pl.ds(other * half, half)
    loads = [
        pltpu.make_async_copy(blocks_in.at[0, own_rows], xin.at[sec], load_sem.at[0]),
        pltpu.make_async_copy(down_in.at[0], wd.at[sec], load_sem.at[1]),
        pltpu.make_async_copy(up_in.at[0], wu.at[sec], load_sem.at[2]),
        pltpu.make_async_copy(enc_in, ek, load_sem.at[3]),
        pltpu.make_async_copy(dec_in, dk, load_sem.at[4]),
        pltpu.make_async_copy(cot_in.at[own_rows], cot.at[0], load_sem.at[5]),
    ]
    for load in loads:
        load.start()
    vec[...] = jnp.zeros_like(vec)
    for at, ref in enumerate((in_gain, in_shift, up_bias)):
        vec[sec, at : at + 1, :] = ref[...]
    for at, ref in enumerate((down_bias, mid_gain, mid_shift, conv_bias, out_gain, out_shift)):
        vec[sec, 3 + at : 4 + at, :inner] = ref[...]
    vsum[...] = jnp.zeros_like(vsum)

    known = {}

    def place(stage):
        if stage not in known:
            axis, strides, radix = stage
            index = lax.axis_index(axis)
            stride = strides[0] if strides[0] == strides[1] else jnp.where(sec == 0, *strides)
            digit = lax.rem(lax.div(index, stride), radix)
            others = [
                {axis: index + (lax.rem(digit + step, radix) - digit) * stride}
                for step in range(1, radix)
            ]
            known[stage] = digit, others
        return known[stage]

    greeted = [peer for stage in plan.vec_stages for peer in place(stage)[1]]
    barrier = pltpu.get_barrier_semaphore()
    for peer in greeted:
        pl.semaphore_signal(barrier, inc=1, device_id=peer, device_id_type=MESH)
    pl.semaphore_wait(barrier, len(greeted))

    pair = [
        remote(blocks_in.at[0, other_rows], xin.at[sec], pair_send.at[0], pair_recv.at[0], other_core),
        remote(vec.at[sec], vec.at[sec], pair_send.at[1], pair_recv.at[1], other_core),
        remote(down_in.at[0], wd.at[sec], pair_send.at[2], pair_recv.at[2], other_core),
        remote(up_in.at[0], wu.at[sec], pair_send.at[3], pair_recv.at[3], other_core),
    ]
    arriving = [
        remote(ref.at[other], ref.at[other], pair_send.at[at], pair_recv.at[at], other_core)
        for at, ref in enumerate((xin, vec, wd, wu))
    ]
    for copy in pair:
        copy.start()
    later_sends.extend(pair)
    seg_copies = [
        remote(seg_in, seg_side.at[0], seg_send.at[0], seg_recv.at[0], right),
        remote(seg_in, seg_side.at[1], seg_send.at[1], seg_recv.at[1], left),
    ]
    for copy in seg_copies:
        copy.start()
    later_sends.extend(seg_copies)

    def wait_block(block):
        @pl.when(sec == block)
        def _():
            for load in loads[:3]:
                load.wait()

        @pl.when(sec != block)
        def _():
            for copy in arriving:
                copy.wait_recv()

    def build_masks():
        for copy in seg_copies:
            copy.wait_recv()
        ext = plan.ext
        position = lax.broadcasted_iota(jnp.int32, (ext, length), 0)
        token = lax.broadcasted_iota(jnp.int32, (ext, length), 1)
        for row in range(half):
            at = pl.ds(sec * half + row, 1)
            own = (seg_in[at, :] + 1).astype(F32)
            before = jnp.where(seq > 0, (seg_side[0, at, :] + 1).astype(F32), 0.0)
            after = jnp.where(seq < plan.n_seq - 1, (seg_side[1, at, :] + 1).astype(F32), 0.0)
            numbers = jnp.where(position - MARGIN == token, own, 0.0)
            numbers = numbers + jnp.where(position + (length - MARGIN) == token, before, 0.0)
            numbers = numbers + jnp.where(position - (length + MARGIN) == token, after, 0.0)
            numbers = dot(numbers.astype(BF16), jnp.ones((length, 128), BF16), 1, 0)
            here = numbers[MARGIN : MARGIN + length]
            for at_offset, offset in enumerate(OFFSETS):
                there = numbers[MARGIN + offset : MARGIN + offset + length]
                masks[at_offset, row] = jnp.where(there == here, 1.0, 0.0).astype(BF16)

    edges = [span for row in range(half) for span in ((row, 0, MARGIN), (row, length - MARGIN, length))]
    middle = [(row, MARGIN, length - MARGIN) for row in range(half)]
    everywhere = [(row, 0, length) for row in range(half)]

    def take(ref, at, part, offset=0):
        return jnp.concatenate(
            [ref[at, row, low + offset : high + offset, :] for row, low, high in part], axis=0
        )

    def put(ref, at, part, value, offset=0):
        done = 0
        for row, low, high in part:
            ref[at, row, low + offset : high + offset, :] = value[done : done + high - low]
            done += high - low

    def window(ref, block, offset):
        piece = take(ref, block, everywhere, MARGIN + offset)
        if offset == 0:
            return piece
        return piece * across(take(masks, OFFSETS.index(offset), everywhere), inner)

    def params(block):
        wide = [vec[block, at : at + 1, :] for at in range(3)]
        narrow = [vec[block, 3 + at : 4 + at, :inner] for at in range(6)]
        return wide + narrow

    def halo(ref, which, block):
        copies = []
        for row in range(half):
            if block == 0 or which == 0:
                copies.append(remote(
                    ref.at[block, row, pl.ds(length, MARGIN)], ref.at[block, row, pl.ds(0, MARGIN)],
                    halo_send.at[which, block, row, 0], halo_recv.at[which, block, row, 0], right,
                ))
            if block == 0 or which == 1:
                copies.append(remote(
                    ref.at[block, row, pl.ds(MARGIN, MARGIN)],
                    ref.at[block, row, pl.ds(length + MARGIN, MARGIN)],
                    halo_send.at[which, block, row, 1], halo_recv.at[which, block, row, 1], left,
                ))
        return copies

    def entry(block, part):
        values = take(xin, block, part).astype(F32)
        if block == 1:
            values = values + take(outv, 0, part).astype(F32)
        return values

    def spread(factor):
        return jnp.broadcast_to(factor, (factor.shape[0], 128))

    def forward_in(block):
        p = params(block)
        for part in (edges, middle):
            normed, factor, act, slope = norm_act(entry(block, part), p[0], p[1])
            put(n1, block, part, normed)
            put(s1, block, part, slope)
            put(q1, block, part, spread(factor))
            act = act.astype(BF16)
            put(fa, block, part, act)
            hidden = dot(act, wd[block], 1, 1) + p[3]
            normed, factor, act, slope = norm_act(hidden, p[4], p[5])
            put(n2, block, part, normed)
            put(s2, block, part, slope)
            put(q2, block, part, spread(factor))
            put(mid, block, part, act.astype(BF16), MARGIN)
            if part is edges:
                for copy in halo(mid, 0, block):
                    copy.start()

    def forward_out(block):
        p = params(block)
        for copy in halo(mid, 0, block):
            copy.wait()
        total = None
        for tap in range(plan.taps[block]):
            piece = window(mid, block, (tap - 2) * DILATION)
            put(win, block * plan.taps[0] + tap, everywhere, piece)
            term = dot(piece, kernels[block][tap], 1, 0)
            total = term if total is None else total + term
        normed, factor, act, slope = norm_act(total + p[6], p[7], p[8])
        put(n3, block, everywhere, normed)
        put(s3, block, everywhere, slope)
        put(q3, block, everywhere, spread(factor))
        act = act.astype(BF16)
        put(la, block, everywhere, act)
        result = entry(block, everywhere) + dot(act, wu[block], 1, 0) + p[2]
        put(outv, block, everywhere, result.astype(BF16))

    def add_wide(block, at, value):
        vsum[block, at : at + 1, :] += value[:, :512]
        vsum[block, at + 1 : at + 2, : width - 512] += value[:, 512:]

    def add_narrow(block, at, value):
        vsum[block, at : at + 1, :inner] += value

    def upstream_of(block, part):
        return take(cot, 0, part) if block == 1 else take(gin, 1, part)

    def last_grad(block):
        incoming = upstream_of(block, everywhere)
        add_wide(block, 4, jnp.sum(incoming.astype(F32), axis=0, keepdims=True))
        put(dl, 0, everywhere, dot(incoming, wu[block], 1, 1))

    def backward_out(block):
        p = params(block)
        for part in (edges, middle):
            if block == 1:
                d_last = take(dl, 0, part)
            else:
                incoming = upstream_of(block, part)
                add_wide(block, 4, jnp.sum(incoming.astype(F32), axis=0, keepdims=True))
                d_last = dot(incoming, wu[block], 1, 1)
            d_conv, gain_grad, shift_grad = norm_act_back(
                d_last, take(s3, block, part), take(n3, block, part),
                across(take(q3, block, part), inner), p[7],
            )
            add_narrow(block, 10, gain_grad)
            add_narrow(block, 11, shift_grad)
            add_narrow(block, 9, jnp.sum(d_conv, axis=0, keepdims=True))
            put(cp, block, part, d_conv.astype(BF16), MARGIN)
            if part is edges:
                for copy in halo(cp, 1, block):
                    copy.start()

    def backward_mid(block):
        p = params(block)
        for copy in halo(cp, 1, block):
            copy.wait()
        total = None
        for tap in range(plan.taps[block]):
            term = dot(window(cp, block, -(tap - 2) * DILATION), kernels[block][tap], 1, 1)
            total = term if total is None else total + term
        d_hidden, gain_grad, shift_grad = norm_act_back(
            total, take(s2, block, everywhere), take(n2, block, everywhere),
            across(take(q2, block, everywhere), inner), p[4],
        )
        add_narrow(block, 7, gain_grad)
        add_narrow(block, 8, shift_grad)
        add_narrow(block, 6, jnp.sum(d_hidden, axis=0, keepdims=True))
        put(hp, block, everywhere, d_hidden.astype(BF16))

    def backward_in(block):
        p = params(block)
        d_first = dot(take(hp, block, everywhere), wd[block], 1, 0)
        d_entry, gain_grad, shift_grad = norm_act_back(
            d_first, take(s1, block, everywhere), take(n1, block, everywhere),
            across(take(q1, block, everywhere), width), p[0],
        )
        add_wide(block, 0, gain_grad)
        add_wide(block, 2, shift_grad)
        incoming = upstream_of(block, everywhere).astype(F32)
        put(gin, block, everywhere, (incoming + d_entry).astype(BF16))

    def to_pool(position, left_value, right_value):
        rows, columns = left_value.shape[1], right_value.shape[1]
        main, rest = divmod(columns, 128)
        product = dot(left_value, right_value[:, : main * 128], 0, 0).astype(BF16)
        for tile in range(main):
            pool[position + tile * rows : position + (tile + 1) * rows, :] = product[
                :, tile * 128 : (tile + 1) * 128
            ]
        position += main * rows
        product = dot(right_value[:, main * 128 :], left_value, 0, 0).astype(BF16)
        for tile in range(-(-rows // 128)):
            lanes = min(128, rows - tile * 128)
            pool[position + tile * rest : position + (tile + 1) * rest, :lanes] = product[
                :, tile * 128 : tile * 128 + lanes
            ]

    def up_weight_grad(block):
        to_pool(plan.at["up", block], take(la, block, everywhere), upstream_of(block, everywhere))

    def kernel_grad(block, tap):
        to_pool(
            plan.at["kernel", block] + tap * plan.tap_rows,
            take(win, block * plan.taps[0] + tap, everywhere), take(cp, block, everywhere, MARGIN),
        )

    def down_weight_grad(block):
        to_pool(plan.at["down", block], take(hp, block, everywhere), take(fa, block, everywhere))

    pool_copies, running = [], {}

    def sum_chunk(chunk):
        first, last, stages = plan.chunks[chunk]
        places = [place(stage) for stage in stages]
        sizes, offsets = [last - first], [first]
        for (digit, _), (_, _, radix) in zip(places, stages):
            sizes.append(sizes[-1] // radix)
            offsets.append(pl.multiple_of(offsets[-1] + digit * sizes[-1], 16))

        def part(ref, stage, digit):
            size = sizes[stage + 1]
            return ref.at[pl.ds(pl.multiple_of(offsets[stage] + digit * size, 16), size)]

        for stage, (_, _, radix) in enumerate(stages):
            digit, others = places[stage]
            size, landing = sizes[stage + 1], plan.landing[chunk][stage]
            sem = rs_recv.at[chunk * plan.most_stages + stage]
            for step in range(1, radix):
                remote(
                    part(pool, stage, lax.rem(digit + step, radix)),
                    recv.at[pl.ds(landing + (step - 1) * size, size)],
                    pool_send.at[0], sem, others[step - 1],
                ).start()
            yield
            landed = recv.at[pl.ds(landing, (radix - 1) * size)]
            remote(landed, landed, pool_send.at[0], sem, others[0]).wait_recv()
            target = summed if stage + 1 == len(stages) else pool
            block = row_block(size)

            def add(at, carry):
                own = pl.ds(pl.multiple_of(offsets[stage + 1] + at * block, 16), block)
                total = pool[own, :].astype(F32)
                for step in range(radix - 1):
                    from_row = pl.multiple_of(landing + step * size + at * block, 16)
                    total = total + recv[pl.ds(from_row, block), :].astype(F32)
                target[own, :] = total.astype(BF16)
                return carry

            lax.fori_loop(0, size // block, add, 0)
        for stage in reversed(range(len(stages))):
            radix = stages[stage][2]
            digit, others = places[stage]
            size = sizes[stage + 1]
            sem = ag_recv.at[chunk * plan.most_stages + stage]
            own = part(summed, stage, digit)
            for step in range(1, radix):
                remote(own, own, pool_send.at[1], sem, others[step - 1]).start()
            yield
            arriving = summed.at[pl.ds(first, (radix - 1) * size)]
            remote(arriving, arriving, pool_send.at[1], sem, others[0]).wait_recv()
        whole = pl.ds(first, last - first)
        copy = pltpu.make_async_copy(summed.at[whole], pool_out.at[whole], out_sem.at[chunk])
        copy.start()
        pool_copies.append(copy)

    def sum_vectors():
        total, slot = None, 0
        for at, stage in enumerate(plan.vec_stages):
            digit, others = place(stage)
            count = stage[2] - 1
            for step in range(count):
                source = vsum.at[other] if at == 0 else vtotal.at[at - 1]
                remote(
                    source, vrecv.at[slot + step], vec_send.at[0], vec_recv.at[at], others[step]
                ).start()
            yield
            landed = vrecv.at[pl.ds(slot, count)]
            remote(landed, landed, vec_send.at[0], vec_recv.at[at], others[0]).wait_recv()
            total = vsum[sec] if at == 0 else vtotal[at - 1]
            for step in range(count):
                total = total + vrecv[slot + step]
            vtotal[at] = total
            slot += count

    def tick(which):
        if which not in running:
            running[which] = sum_vectors() if which == VECTORS else sum_chunk(which)
        if running[which] is not None and next(running[which], "done") == "done":
            running[which] = None

    def run(steps):
        for step in steps:
            if isinstance(step, int):
                if step == VECTORS or plan.chunks[step][0] < plan.chunks[step][1]:
                    tick(step)
            else:
                step[0](*step[1:])

    results = []

    def send_result(at):
        value, result = ((outv, blocks_out), (gin, grads_out))[at]
        for row in range(half):
            target = result.at[0, sec * half + row]
            landing = result.at[0, other * half + row]
            local = pltpu.make_async_copy(value.at[sec, row], target, out_send.at[0, at, row])
            sems = out_send.at[1, at, row], out_recv.at[at, row]
            away = remote(value.at[other, row], target, *sems, other_core)
            local.start()
            away.start()
            results.append((local, away, remote(value.at[other, row], landing, *sems, other_core)))

    wait_block(0)
    forward_in(0)
    build_masks()
    loads[3].wait()
    forward_out(0)
    wait_block(1)
    forward_in(1)
    loads[5].wait()
    last_grad(1)
    loads[4].wait()
    forward_out(1)
    send_result(0)
    if plan.pool_rows > plan.used_rows:
        pool[plan.used_rows : plan.pool_rows, :] = jnp.zeros(
            (plan.pool_rows - plan.used_rows, 128), BF16
        )
    run((
        (backward_out, 1), (up_weight_grad, 1), (kernel_grad, 1, 0), 0, (backward_mid, 1), (kernel_grad, 1, 2), 0, (down_weight_grad, 1), (kernel_grad, 1, 1), 2, (backward_in, 1), 2, (backward_out, 0), 0, 1, (kernel_grad, 0, 0), (up_weight_grad, 0), (kernel_grad, 0, 1), 3, 1, (kernel_grad, 0, 2), (kernel_grad, 0, 3), 2, 5, 0, 3, (backward_mid, 0), 2, 1, 5, (down_weight_grad, 0), 0, (kernel_grad, 0, 4), 7, 3, 1, 7, 2, 5, 3, 0, 6, 4, 6, 1, 7, 4, 5, 0, 2, 3, 1, 7, 6, 4, 2, 5, 3, 4, 6, 7, 1, 5, 3, 4, 6, 2, 7, 0, 2, 1, 5, 6, 4, 0, 1, 7, 3, 4, 5, 6, (backward_in, 0), (send_result, 1), VECTORS, 7, 4, 6, 5, 3, 7, 4, 6,
    ))

    while any(events is not None for events in running.values()):
        run(tuple(range(len(plan.chunks))) + (VECTORS,))
    vec_out[...] = vtotal[len(plan.vec_stages) - 1]
    for local, away, arrives in results:
        local.wait()
        away.wait_send()
        arrives.wait_recv()
    for copy in pool_copies:
        copy.wait()
    for copy in later_sends:
        copy.wait_send()
    for at in range(2):
        everything = summed.at[pl.ds(0, plan.sent_rows)]
        remote(everything, everything, pool_send.at[at], rs_recv.at[0], other_core).wait_send()
    remote(vrecv, vrecv, vec_send.at[0], vec_recv.at[0], other_core).wait_send()


def final_kernel(plan, blocks_in, grads_in, pool_in, vec, *refs):
    (
        blocks_out, grads_out, g_in_gain, g_in_shift, g_down, g_down_bias, g_mid_gain, g_mid_shift,
        g_enc, g_dec, g_conv_bias, g_out_gain, g_out_shift, g_up, g_up_bias,
        bounce, up_pool, down_pool, tap_pool, up_full, down_full, enc_full, dec_full,
        in_sem, out_sem,
    ) = refs
    sec = lax.axis_index("section")
    width, inner = plan.width, plan.inner
    entering = [
        pltpu.make_async_copy(blocks_in, bounce.at[0], in_sem.at[4]),
        pltpu.make_async_copy(grads_in, bounce.at[1], in_sem.at[5]),
    ]
    passed = [
        pltpu.make_async_copy(bounce.at[0], blocks_out, out_sem.at[0]),
        pltpu.make_async_copy(bounce.at[1], grads_out, out_sem.at[1]),
    ]
    for copy in entering:
        copy.start()

    def load(name, target, size, sem):
        start = jnp.where(sec == 0, plan.at[name, 0], plan.at[name, 1])
        copy = pltpu.make_async_copy(pool_in.at[pl.ds(pl.multiple_of(start, 16), size)], target, in_sem.at[sem])
        copy.start()
        return copy

    up_load = load("up", up_pool, plan.up_rows, 0)
    down_load = load("down", down_pool, plan.down_rows, 1)
    tap_loads = []
    at = 0
    for block in (0, 1):
        size = plan.tap_rows * plan.taps[block]
        start = plan.at["kernel", block]
        copy = pltpu.make_async_copy(pool_in.at[pl.ds(start, size)], tap_pool.at[pl.ds(at, size)], in_sem.at[2 + block])
        copy.start()
        tap_loads.append(copy)
        at += size

    def wide(at):
        return jnp.concatenate([vec[at : at + 1, :], vec[at + 1 : at + 2, : width - 512]], axis=1)

    g_in_gain[...] = wide(0)
    g_in_shift[...] = wide(2)
    g_up_bias[...] = wide(4)
    for at, ref in enumerate((g_down_bias, g_mid_gain, g_mid_shift, g_conv_bias, g_out_gain, g_out_shift)):
        ref[...] = vec[6 + at : 7 + at, :inner]

    def rest_of(ref, position, rest, tiles):
        pieces = [ref[position + tile * rest : position + (tile + 1) * rest, :] for tile in range(tiles)]
        return jnp.concatenate(pieces, axis=1).astype(F32)

    def unpack(ref, full, rows, main, rest, tiles):
        for tile in range(main):
            full[:, tile * 128 : (tile + 1) * 128] = ref[tile * rows : (tile + 1) * rows, :].astype(F32)
        left = rest_of(ref, main * rows, rest, tiles)
        full[:, main * 128 :] = left.T[:rows, :]

    for first, second in zip(entering, passed):
        first.wait()
        second.start()
    up_load.wait()
    unpack(up_pool, up_full, inner, plan.up_main, plan.up_rest, plan.in_tiles)
    up_store = pltpu.make_async_copy(up_full, g_up.at[0], out_sem.at[2])
    up_store.start()
    down_load.wait()
    unpack(down_pool, down_full, inner, plan.up_main, plan.up_rest, plan.in_tiles)
    down_store = pltpu.make_async_copy(down_full, g_down.at[0], out_sem.at[3])
    down_store.start()
    part = inner // 2
    row = lax.broadcasted_iota(jnp.int32, (inner, part), 0)
    column = lax.broadcasted_iota(jnp.int32, (inner, part), 1)
    choose = jnp.where(row == column + sec * part, 1.0, 0.0).astype(BF16)
    stores = []
    at = 0
    for block, full, target in ((0, enc_full, g_enc), (1, dec_full, g_dec)):
        tap_loads[block].wait()
        for tap in range(plan.taps[block]):
            main = jnp.concatenate(
                [tap_pool[at + tile * inner : at + (tile + 1) * inner, :] for tile in range(plan.in_main)], axis=1
            )
            lanes = plan.in_main * 128
            rest = rest_of(tap_pool, at + plan.in_main * inner, plan.in_rest, plan.in_tiles)
            rest = rest[:, :inner].astype(BF16)
            full[tap] = dot(main, choose[:lanes], 1, 0) + dot(rest, choose[lanes:], 0, 0)
            at += plan.tap_rows
        copy = pltpu.make_async_copy(full, target, out_sem.at[4 + block])
        copy.start()
        stores.append(copy)
    for copy in passed + [up_store, down_store] + stores:
        copy.wait()


def per_device(plan, *args):
    (
        block_inputs, cotangent, segment_ids, in_gain, in_shift, down_weight, down_bias, mid_gain,
        mid_shift, enc_kernel, dec_kernel, conv_bias, out_gain, out_shift, up_weight, up_bias,
    ) = args
    args = args[:5] + (jnp.swapaxes(down_weight, 1, 2),) + args[6:]
    length, width, inner, half, tokens = plan.length, plan.width, plan.inner, plan.half, plan.tokens
    chunks = len(plan.chunks)
    any_spec = pl.BlockSpec(memory_space=pl.ANY)
    vmem_spec = pl.BlockSpec(memory_space=pltpu.VMEM)
    wide = lambda kind: pltpu.VMEM((2, half, length, width), kind)
    narrow = lambda kind: pltpu.VMEM((2, half, length, inner), kind)
    factor = pltpu.VMEM((2, half, length, 128), F32)
    dma = pltpu.SemaphoreType.DMA
    enc_taps, dec_taps = plan.taps
    blocks, grads, pool, vectors = pl.pallas_call(
        functools.partial(main_kernel, plan),
        out_shape=(
            jax.ShapeDtypeStruct(block_inputs.shape, BF16),
            jax.ShapeDtypeStruct(block_inputs.shape, BF16),
            jax.ShapeDtypeStruct((plan.pool_rows, 128), BF16),
            jax.ShapeDtypeStruct((16, 512), F32),
        ),
        in_specs=[any_spec, any_spec, vmem_spec, vmem_spec, vmem_spec, any_spec, vmem_spec, vmem_spec,
                  vmem_spec, any_spec, any_spec, vmem_spec, vmem_spec, vmem_spec, any_spec, vmem_spec],
        out_specs=(any_spec, any_spec, any_spec, vmem_spec),
        scratch_shapes=[
            pltpu.VMEM((2, half, length, width), BF16),
            pltpu.VMEM((1, half, length, width), BF16),
            pltpu.VMEM((2, inner, width), BF16),
            pltpu.VMEM((2, inner, width), BF16),
            pltpu.VMEM((enc_taps, inner, inner), BF16),
            pltpu.VMEM((dec_taps, inner, inner), BF16),
            pltpu.VMEM((2, 16, width), F32),
            pltpu.VMEM((2,) + segment_ids.shape, jnp.int32),
            pltpu.VMEM((len(OFFSETS), half, length, 128), BF16),
            wide(F32), wide(F32), factor,
            narrow(F32), narrow(F32), factor,
            narrow(F32), narrow(F32), factor,
            wide(BF16),
            pltpu.VMEM((2, half, plan.ext, inner), BF16),
            pltpu.VMEM((enc_taps + dec_taps, half, length, inner), BF16),
            narrow(BF16),
            wide(BF16),
            pltpu.VMEM((2, half, plan.ext, inner), BF16),
            narrow(BF16),
            wide(BF16),
            pltpu.VMEM((1, half, length, inner), F32),
            pltpu.VMEM((plan.pool_rows, 128), BF16),
            pltpu.VMEM((plan.pool_rows, 128), BF16),
            pltpu.VMEM((plan.recv_rows, 128), BF16),
            pltpu.VMEM((2, 16, 512), F32),
            pltpu.VMEM((len(plan.vec_stages), 16, 512), F32),
            pltpu.VMEM((plan.vec_copies, 16, 512), F32),
            dma((6,)), dma((4,)), dma((4,)), dma((2,)), dma((2,)),
            dma((2, 2, half, 2)), dma((2, 2, half, 2)),
            dma((2,)), dma((chunks * plan.most_stages,)), dma((chunks * plan.most_stages,)),
            dma((1,)), dma((len(plan.vec_stages),)),
            dma((chunks,)), dma((2, 2, half)), dma((2, half)),
        ],
        compiler_params=pltpu.CompilerParams(
            collective_id=0, has_side_effects=True, vmem_limit_bytes=VMEM_LIMIT
        ),
        name="blocks_and_sums",
    )(*args)
    vector = lambda size: jax.ShapeDtypeStruct((1, size), F32)
    part = inner // 2
    results = pl.pallas_call(
        functools.partial(final_kernel, plan),
        out_shape=(
            jax.ShapeDtypeStruct(block_inputs.shape, BF16),
            jax.ShapeDtypeStruct(block_inputs.shape, BF16),
            vector(width), vector(width),
            jax.ShapeDtypeStruct((1, inner, width), F32),
            vector(inner), vector(inner), vector(inner),
            jax.ShapeDtypeStruct((enc_taps, inner, part), F32),
            jax.ShapeDtypeStruct((dec_taps, inner, part), F32),
            vector(inner), vector(inner), vector(inner),
            jax.ShapeDtypeStruct((1, inner, width), F32),
            vector(width),
        ),
        in_specs=[any_spec, any_spec, any_spec, vmem_spec],
        out_specs=(any_spec, any_spec, vmem_spec, vmem_spec, any_spec, vmem_spec, vmem_spec, vmem_spec,
                   any_spec, any_spec, vmem_spec, vmem_spec, vmem_spec, any_spec, vmem_spec),
        scratch_shapes=[
            pltpu.VMEM((2,) + block_inputs.shape, BF16),
            pltpu.VMEM((plan.up_rows, 128), BF16),
            pltpu.VMEM((plan.down_rows, 128), BF16),
            pltpu.VMEM((plan.tap_rows * (enc_taps + dec_taps), 128), BF16),
            pltpu.VMEM((inner, width), F32),
            pltpu.VMEM((inner, width), F32),
            pltpu.VMEM((enc_taps, inner, part), F32),
            pltpu.VMEM((dec_taps, inner, part), F32),
            dma((6,)), dma((6,)),
        ],
        compiler_params=pltpu.CompilerParams(vmem_limit_bytes=VMEM_LIMIT),
        name="unpack_sums",
    )(blocks, grads, pool, vectors)
    return results[:4] + (jnp.swapaxes(results[4], 1, 2),) + results[5:]


def solution(mesh):
    def whole(*args):
        rows, length, width = (
            args[0].shape[1] // mesh.shape["dp"], args[0].shape[2] // mesh.shape["seq"], args[0].shape[3]
        )
        inner = args[9].shape[1]
        plan = Plan(mesh, rows, length, width, inner, args[9].shape[0], args[10].shape[0])
        by_section = P("section", None)
        weight = P("section", None, None)
        data = P("section", "dp", "seq", None)
        return jax.shard_map(
            functools.partial(per_device, plan),
            mesh=mesh,
            in_specs=(
                data, P("dp", "seq", None), P("dp", "seq"), by_section, by_section, weight, by_section,
                by_section, by_section, P(), P(), by_section, by_section, by_section, weight, by_section,
            ),
            out_specs=(
                data, data, by_section, by_section, weight, by_section, by_section, by_section,
                P(None, None, "section"), P(None, None, "section"),
                by_section, by_section, by_section, weight, by_section,
            ),
            check_vma=False,
        )(*args)

    return whole
```

```python
import functools

import jax
import jax.numpy as jnp
from jax import lax
from jax.experimental import pallas as pl
from jax.experimental.pallas import tpu as pltpu
from jax.sharding import PartitionSpec as P

DILATION = 16
MARGIN = 2 * DILATION
EPSILON = 1e-05
MESH = pl.DeviceIdType.MESH
BF16 = jnp.bfloat16
F32 = jnp.float32
OFFSETS = (-2 * DILATION, -DILATION, DILATION, 2 * DILATION)
ROOT = 0.7978845608028654
CUBIC = 0.044715 * ROOT
VMEM_LIMIT = 60 * 2**20
VECTORS = -1


def dot(left, right, left_dim, right_dim):
    return lax.dot_general(
        left, right, (((left_dim,), (right_dim,)), ((), ())), preferred_element_type=F32
    )


def across(column, width):
    whole, rest = divmod(width, 128)
    pieces = [column] * whole
    if rest:
        pieces.append(column[:, :rest])
    return jnp.concatenate(pieces, axis=1) if len(pieces) > 1 else pieces[0]


def norm_act(values, gain, shift):
    scale = 1.0 / values.shape[-1]
    centred = values - jnp.sum(values, axis=-1, keepdims=True) * scale
    variance = jnp.sum(centred * centred, axis=-1, keepdims=True) * scale
    factor = lax.rsqrt(variance + EPSILON)
    normed = centred * factor
    pre = normed * gain + shift
    square = pre * pre
    half = 0.5 + 0.5 * jnp.tanh(pre * (ROOT + CUBIC * square))
    act = pre * half
    slope = half + act * (1.0 - half) * (2.0 * ROOT + 6.0 * CUBIC * square)
    return normed, factor, act, slope


def norm_act_back(upstream, slope, normed, factor, gain):
    scale = 1.0 / normed.shape[-1]
    at_pre = upstream * slope
    shift_grad = jnp.sum(at_pre, axis=0, keepdims=True)
    gain_grad = jnp.sum(at_pre * normed, axis=0, keepdims=True)
    scaled = at_pre * gain
    first = jnp.sum(scaled, axis=-1, keepdims=True) * scale
    second = jnp.sum(scaled * normed, axis=-1, keepdims=True) * scale
    return factor * (scaled - first - normed * second), gain_grad, shift_grad


def row_block(rows):
    best = 16
    for size in range(16, 257, 16):
        if rows % size == 0:
            best = size
    return best


PARTS = 40
CHUNKS = ((4, "std"), (11, "std"), (17, "std"), (19, "std"), (23, "std"), (29, "std"), (34, "std"), (38, "std"), (40, "std"))


class Plan:
    def __init__(self, mesh, rows, length, width, inner, enc_taps, dec_taps):
        self.rows, self.length, self.width, self.inner = rows, length, width, inner
        self.half = rows // 2
        self.tokens = self.half * length
        self.taps = (enc_taps, dec_taps)
        self.n_dp, self.n_seq = mesh.shape["dp"], mesh.shape["seq"]
        self.ext = length + 2 * MARGIN
        self.up_main, self.up_rest = divmod(width, 128)
        self.in_main, self.in_rest = divmod(inner, 128)
        lanes = lambda size: -(-size // 128)
        self.in_tiles, self.width_tiles = lanes(inner), lanes(width)
        self.up_rows = self.up_main * inner + self.up_rest * self.in_tiles
        self.down_rows = self.up_rows
        self.tap_rows = self.in_main * inner + self.in_rest * self.in_tiles
        self.tap_part = self.tap_rows - inner // 2 // 128 * inner
        position = 0
        self.at = {}
        for name, block, size, pieces in (
            ("up", 1, self.up_rows, 1), ("kernel", 1, self.tap_rows, dec_taps), ("down", 1, self.down_rows, 1),
            ("up", 0, self.up_rows, 1), ("kernel", 0, self.tap_rows, enc_taps), ("down", 0, self.down_rows, 1),
        ):
            self.at[name, block] = position
            position += size * pieces
        self.used_rows = position
        section = [("section", (1, 1), 2)]
        bits = self.n_seq.bit_length() - 1
        assert self.n_seq == 1 << bits
        halves = [("seq", (1 << bit, 1 << (bits - 1 - bit)), 2) for bit in range(bits)]
        direct = [("seq", (1, 1), self.n_seq)] if bits else []
        layers, left, stride = [], self.n_dp, 1
        while left > 1:
            radix = 4 if left % 4 == 0 else 2
            assert left % radix == 0
            layers.append(("dp", (stride, stride), radix))
            left, stride = left // radix, stride * radix
        orders = {"std": section + halves + layers, "dp first": section + layers + halves,
                  "direct": section + direct + layers}
        self.vec_stages = orders["direct"]
        unit = 32 * self.n_seq * self.n_dp
        self.pool_rows = -(-self.used_rows // unit) * unit
        nominal = -(-self.used_rows // 512) * 512
        self.chunks, first = [], 0
        for end, order in CHUNKS:
            last = self.pool_rows if end == PARTS else nominal * end // PARTS // unit * unit
            self.chunks.append((first, last, orders[order]))
            first = last
        self.landing, self.recv_rows = [], 0
        for first, last, stages in self.chunks:
            size, places = last - first, []
            for _, _, radix in stages:
                size //= radix
                places.append(self.recv_rows)
                self.recv_rows += size * (radix - 1)
            self.landing.append(places)
        self.sent_rows = self.pool_rows - self.pool_rows // (unit // 16)
        self.most_stages = max(len(stages) for _, _, stages in self.chunks)
        self.vec_copies = sum(radix - 1 for _, _, radix in self.vec_stages)


def main_kernel(plan, *refs):
    (
        blocks_in, cot_in, seg_in, in_gain, in_shift, down_in, down_bias, mid_gain, mid_shift,
        enc_in, dec_in, conv_bias, out_gain, out_shift, up_in, up_bias,
        blocks_out, grads_out, pool_out, vec_out,
        xin, cot, wd, wu, ek, dk, vec, seg_side, masks,
        n1, s1, q1, n2, s2, q2, n3, s3, q3, fa, mid, win, la, outv, cp, hp, gin, dl,
        pool, summed, recv, vsum, vtotal, vrecv, halo_bytes,
        load_sem, pair_send, pair_recv, seg_send, seg_recv, halo_send, halo_recv,
        pool_send, rs_recv, ag_recv, vec_send, vec_recv, out_sem, out_send, out_recv,
    ) = refs
    length, width, inner, half = plan.length, plan.width, plan.inner, plan.half
    kernels = (ek, dk)
    sec = lax.axis_index("section")
    seq = lax.axis_index("seq")
    other = 1 - sec
    other_core = {"section": other}
    right = {"seq": lax.rem(seq + 1, plan.n_seq)}
    left = {"seq": lax.rem(seq + plan.n_seq - 1, plan.n_seq)}
    later_sends = []

    def remote(src, dst, send, recv, device):
        return pltpu.make_async_remote_copy(
            src_ref=src, dst_ref=dst, send_sem=send, recv_sem=recv,
            device_id=device, device_id_type=MESH,
        )

    own_rows = pl.ds(sec * half, half)
    loads = [
        pltpu.make_async_copy(blocks_in.at[0, own_rows], xin.at[sec], load_sem.at[0]),
        pltpu.make_async_copy(down_in.at[0], wd.at[sec], load_sem.at[1]),
        pltpu.make_async_copy(up_in.at[0], wu.at[sec], load_sem.at[2]),
        pltpu.make_async_copy(enc_in, ek, load_sem.at[3]),
        pltpu.make_async_copy(dec_in, dk, load_sem.at[4]),
        pltpu.make_async_copy(cot_in.at[own_rows], cot.at[0], load_sem.at[5]),
    ]
    loads[0].start()
    loads[1].start()
    vec[...] = jnp.zeros_like(vec)
    for at, ref in enumerate((in_gain, in_shift, up_bias)):
        vec[sec, at : at + 1, :] = ref[...]
    for at, ref in enumerate((down_bias, mid_gain, mid_shift, conv_bias, out_gain, out_shift)):
        vec[sec, 3 + at : 4 + at, :inner] = ref[...]

    known = {}

    def place(stage):
        if stage not in known:
            axis, strides, radix = stage
            index = lax.axis_index(axis)
            stride = strides[0] if strides[0] == strides[1] else jnp.where(sec == 0, *strides)
            digit = lax.rem(lax.div(index, stride), radix)
            others = [
                {axis: index + (lax.rem(digit + step, radix) - digit) * stride}
                for step in range(1, radix)
            ]
            known[stage] = digit, others
        return known[stage]

    greeted = [peer for stage in plan.vec_stages for peer in place(stage)[1]]
    barrier = pltpu.get_barrier_semaphore()
    for peer in greeted:
        pl.semaphore_signal(barrier, inc=1, device_id=peer, device_id_type=MESH)
    pl.semaphore_wait(barrier, len(greeted))

    def pair(src, dst, at):
        copy = remote(src, dst, pair_send.at[at], pair_recv.at[at], other_core)
        copy.start()
        return copy

    def pair_rows(at, low, size):
        for row in range(half):
            rows = pl.ds(low, size)
            pair(blocks_in.at[0, other * half + row, rows], xin.at[sec, row, rows], at)

    pair(vec.at[sec], vec.at[sec], 0)
    pair_rows(1, 0, MARGIN)
    pair_rows(1, length - MARGIN, MARGIN)
    pair(down_in.at[0], wd.at[sec], 2)
    pair_rows(3, MARGIN, length - 2 * MARGIN)
    pair(up_in.at[0], wu.at[sec], 4)
    pair_whole = (
        vec.at[other], xin.at[other, :, pl.ds(0, 2 * MARGIN)], wd.at[other],
        xin.at[other, :, pl.ds(0, length - 2 * MARGIN)], wu.at[other],
    )
    arriving = [
        remote(ref, ref, pair_send.at[at], pair_recv.at[at], other_core)
        for at, ref in enumerate(pair_whole)
    ]
    later_sends.extend(arriving)
    seg_copies = [
        remote(seg_in, seg_side.at[0], seg_send.at[0], seg_recv.at[0], right),
        remote(seg_in, seg_side.at[1], seg_send.at[1], seg_recv.at[1], left),
    ]
    for copy in seg_copies:
        copy.start()
    later_sends.extend(seg_copies)
    for load in loads[2:]:
        load.start()
    vsum[...] = jnp.zeros_like(vsum)

    def wait_pair(block, local, away):
        @pl.when(sec == block)
        def _():
            for at in local:
                loads[at].wait()

        @pl.when(sec != block)
        def _():
            for at in away:
                arriving[at].wait_recv()

    def build_masks():
        for copy in seg_copies:
            copy.wait_recv()
        ext = plan.ext
        position = lax.broadcasted_iota(jnp.int32, (ext, length), 0)
        token = lax.broadcasted_iota(jnp.int32, (ext, length), 1)
        for row in range(half):
            at = pl.ds(sec * half + row, 1)
            own = (seg_in[at, :] + 1).astype(F32)
            before = jnp.where(seq > 0, (seg_side[0, at, :] + 1).astype(F32), 0.0)
            after = jnp.where(seq < plan.n_seq - 1, (seg_side[1, at, :] + 1).astype(F32), 0.0)
            numbers = jnp.where(position - MARGIN == token, own, 0.0)
            numbers = numbers + jnp.where(position + (length - MARGIN) == token, before, 0.0)
            numbers = numbers + jnp.where(position - (length + MARGIN) == token, after, 0.0)
            numbers = dot(numbers.astype(BF16), jnp.ones((length, 128), BF16), 1, 0)
            here = numbers[MARGIN : MARGIN + length]
            for at_offset, offset in enumerate(OFFSETS):
                there = numbers[MARGIN + offset : MARGIN + offset + length]
                masks[at_offset, row] = jnp.where(there == here, 1.0, 0.0).astype(BF16)

    edges = [span for row in range(half) for span in ((row, 0, MARGIN), (row, length - MARGIN, length))]
    middle = [(row, MARGIN, length - MARGIN) for row in range(half)]
    everywhere = [(row, 0, length) for row in range(half)]

    def take(ref, at, part, offset=0):
        return jnp.concatenate(
            [ref[at, row, low + offset : high + offset, :] for row, low, high in part], axis=0
        )

    def put(ref, at, part, value, offset=0):
        done = 0
        for row, low, high in part:
            ref[at, row, low + offset : high + offset, :] = value[done : done + high - low]
            done += high - low

    def window(ref, block, offset):
        piece = take(ref, block, everywhere, MARGIN + offset)
        if offset == 0:
            return piece
        return piece * across(take(masks, OFFSETS.index(offset), everywhere), inner)

    def params(block):
        wide = [vec[block, at : at + 1, :] for at in range(3)]
        narrow = [vec[block, 3 + at : 4 + at, :inner] for at in range(6)]
        return wide + narrow

    def halo_start(ref, which, block):
        sems = halo_send.at[which, block], halo_recv.at[which, block]
        for row in range(half):
            if block == 0 or which == 0:
                remote(
                    ref.at[block, row, pl.ds(length, MARGIN)], ref.at[block, row, pl.ds(0, MARGIN)],
                    *sems, right,
                ).start()
            if block == 0 or which == 1:
                remote(
                    ref.at[block, row, pl.ds(MARGIN, MARGIN)],
                    ref.at[block, row, pl.ds(length + MARGIN, MARGIN)], *sems, left,
                ).start()

    def halo_wait(which, block):
        count = half * (2 if block == 0 else 1)
        everything = halo_bytes.at[pl.ds(0, count)]
        remote(
            everything, everything, halo_send.at[which, block], halo_recv.at[which, block], right
        ).wait()

    def entry(block, part):
        values = take(xin, block, part).astype(F32)
        if block == 1:
            values = values + take(outv, 0, part).astype(F32)
        return values

    def spread(factor):
        return jnp.broadcast_to(factor, (factor.shape[0], 128))

    def forward_in(block):
        p = params(block)
        for part in (edges, middle):
            if part is middle:
                wait_pair(block, (), (3,))
            normed, factor, act, slope = norm_act(entry(block, part), p[0], p[1])
            put(n1, block, part, normed)
            put(s1, block, part, slope)
            put(q1, block, part, spread(factor))
            act = act.astype(BF16)
            put(fa, block, part, act)
            hidden = dot(act, wd[block], 1, 1) + p[3]
            normed, factor, act, slope = norm_act(hidden, p[4], p[5])
            put(n2, block, part, normed)
            put(s2, block, part, slope)
            put(q2, block, part, spread(factor))
            put(mid, block, part, act.astype(BF16), MARGIN)
            if part is edges:
                halo_start(mid, 0, block)

    def forward_out(block):
        p = params(block)
        halo_wait(0, block)
        total = None
        for tap in range(plan.taps[block]):
            piece = window(mid, block, (tap - 2) * DILATION)
            put(win, block * plan.taps[0] + tap, everywhere, piece)
            term = dot(piece, kernels[block][tap], 1, 0)
            total = term if total is None else total + term
        normed, factor, act, slope = norm_act(total + p[6], p[7], p[8])
        put(n3, block, everywhere, normed)
        put(s3, block, everywhere, slope)
        put(q3, block, everywhere, spread(factor))
        act = act.astype(BF16)
        put(la, block, everywhere, act)
        result = entry(block, everywhere) + dot(act, wu[block], 1, 0) + p[2]
        put(outv, block, everywhere, result.astype(BF16))

    def add_wide(block, at, value):
        vsum[block, at : at + 1, :] += value[:, :512]
        vsum[block, at + 1 : at + 2, : width - 512] += value[:, 512:]

    def add_narrow(block, at, value):
        vsum[block, at : at + 1, :inner] += value

    def upstream_of(block, part):
        return take(cot, 0, part) if block == 1 else take(gin, 1, part)

    def last_grad(block):
        put(dl, 0, everywhere, dot(upstream_of(block, everywhere), wu[block], 1, 1))

    def bias_sum(block):
        incoming = upstream_of(block, everywhere).astype(F32)
        add_wide(block, 4, jnp.sum(incoming, axis=0, keepdims=True))

    def backward_out(block):
        p = params(block)
        for part in (edges, middle):
            if block == 1:
                d_last = take(dl, 0, part)
            else:
                incoming = upstream_of(block, part)
                add_wide(block, 4, jnp.sum(incoming.astype(F32), axis=0, keepdims=True))
                d_last = dot(incoming, wu[block], 1, 1)
            d_conv, gain_grad, shift_grad = norm_act_back(
                d_last, take(s3, block, part), take(n3, block, part),
                across(take(q3, block, part), inner), p[7],
            )
            add_narrow(block, 10, gain_grad)
            add_narrow(block, 11, shift_grad)
            add_narrow(block, 9, jnp.sum(d_conv, axis=0, keepdims=True))
            put(cp, block, part, d_conv.astype(BF16), MARGIN)
            if part is edges:
                halo_start(cp, 1, block)

    def backward_mid(block):
        p = params(block)
        halo_wait(1, block)
        total = None
        for tap in range(plan.taps[block]):
            term = dot(window(cp, block, -(tap - 2) * DILATION), kernels[block][tap], 1, 1)
            total = term if total is None else total + term
        d_hidden, gain_grad, shift_grad = norm_act_back(
            total, take(s2, block, everywhere), take(n2, block, everywhere),
            across(take(q2, block, everywhere), inner), p[4],
        )
        add_narrow(block, 7, gain_grad)
        add_narrow(block, 8, shift_grad)
        add_narrow(block, 6, jnp.sum(d_hidden, axis=0, keepdims=True))
        put(hp, block, everywhere, d_hidden.astype(BF16))

    def backward_in(block):
        p = params(block)
        d_first = dot(take(hp, block, everywhere), wd[block], 1, 0)
        d_entry, gain_grad, shift_grad = norm_act_back(
            d_first, take(s1, block, everywhere), take(n1, block, everywhere),
            across(take(q1, block, everywhere), width), p[0],
        )
        add_wide(block, 0, gain_grad)
        add_wide(block, 2, shift_grad)
        incoming = upstream_of(block, everywhere).astype(F32)
        put(gin, block, everywhere, (incoming + d_entry).astype(BF16))

    def to_pool(position, left_value, right_value):
        rows, columns = left_value.shape[1], right_value.shape[1]
        main, rest = divmod(columns, 128)
        product = dot(left_value, right_value[:, : main * 128], 0, 0).astype(BF16)
        for tile in range(main):
            pool[position + tile * rows : position + (tile + 1) * rows, :] = product[
                :, tile * 128 : (tile + 1) * 128
            ]
        position += main * rows
        product = dot(right_value[:, main * 128 :], left_value, 0, 0).astype(BF16)
        for tile in range(-(-rows // 128)):
            lanes = min(128, rows - tile * 128)
            pool[position + tile * rest : position + (tile + 1) * rest, :lanes] = product[
                :, tile * 128 : tile * 128 + lanes
            ]

    def up_weight_grad(block):
        to_pool(plan.at["up", block], take(la, block, everywhere), upstream_of(block, everywhere))

    def kernel_grad(block, tap):
        to_pool(
            plan.at["kernel", block] + tap * plan.tap_rows,
            take(win, block * plan.taps[0] + tap, everywhere), take(cp, block, everywhere, MARGIN),
        )

    def down_weight_grad(block):
        to_pool(plan.at["down", block], take(hp, block, everywhere), take(fa, block, everywhere))

    running = {}

    def sum_chunk(chunk):
        first, last, stages = plan.chunks[chunk]
        places = [place(stage) for stage in stages]
        sizes, offsets = [last - first], [first]
        for (digit, _), (_, _, radix) in zip(places, stages):
            sizes.append(sizes[-1] // radix)
            offsets.append(pl.multiple_of(offsets[-1] + digit * sizes[-1], 16))

        def part(ref, stage, digit):
            size = sizes[stage + 1]
            return ref.at[pl.ds(pl.multiple_of(offsets[stage] + digit * size, 16), size)]

        for stage, (_, _, radix) in enumerate(stages):
            digit, others = places[stage]
            size, landing = sizes[stage + 1], plan.landing[chunk][stage]
            sem = rs_recv.at[chunk * plan.most_stages + stage]
            for step in range(1, radix):
                remote(
                    part(pool, stage, lax.rem(digit + step, radix)),
                    recv.at[pl.ds(landing + (step - 1) * size, size)],
                    pool_send.at[0], sem, others[step - 1],
                ).start()
            yield
            landed = recv.at[pl.ds(landing, (radix - 1) * size)]
            remote(landed, landed, pool_send.at[0], sem, others[0]).wait_recv()
            target = summed if stage + 1 == len(stages) else pool
            block = row_block(size)

            def add(at, carry):
                own = pl.ds(pl.multiple_of(offsets[stage + 1] + at * block, 16), block)
                total = pool[own, :].astype(F32)
                for step in range(radix - 1):
                    from_row = pl.multiple_of(landing + step * size + at * block, 16)
                    total = total + recv[pl.ds(from_row, block), :].astype(F32)
                target[own, :] = total.astype(BF16)
                return carry

            lax.fori_loop(0, size // block, add, 0)
        for stage in reversed(range(len(stages))):
            radix = stages[stage][2]
            digit, others = places[stage]
            size = sizes[stage + 1]
            sem = ag_recv.at[chunk * plan.most_stages + stage]
            own = part(summed, stage, digit)
            for step in range(1, radix):
                remote(own, own, pool_send.at[1], sem, others[step - 1]).start()
            yield
            arriving = summed.at[pl.ds(first, (radix - 1) * size)]
            remote(arriving, arriving, pool_send.at[1], sem, others[0]).wait_recv()
        whole = pl.ds(first, last - first)
        pltpu.make_async_copy(summed.at[whole], pool_out.at[whole], out_sem.at[0]).start()

    def sum_vectors():
        total, slot = None, 0
        for at, stage in enumerate(plan.vec_stages):
            digit, others = place(stage)
            count = stage[2] - 1
            for step in range(count):
                source = vsum.at[other] if at == 0 else vtotal.at[at - 1]
                remote(
                    source, vrecv.at[slot + step], vec_send.at[0], vec_recv.at[at], others[step]
                ).start()
            yield
            landed = vrecv.at[pl.ds(slot, count)]
            remote(landed, landed, vec_send.at[0], vec_recv.at[at], others[0]).wait_recv()
            total = vsum[sec] if at == 0 else vtotal[at - 1]
            for step in range(count):
                total = total + vrecv[slot + step]
            vtotal[at] = total
            slot += count

    def tick(which):
        if which not in running:
            running[which] = sum_vectors() if which == VECTORS else sum_chunk(which)
        if running[which] is not None and next(running[which], "done") == "done":
            running[which] = None

    def run(steps):
        for step in steps:
            if isinstance(step, int):
                if step == VECTORS or plan.chunks[step][0] < plan.chunks[step][1]:
                    tick(step)
            else:
                step[0](*step[1:])

    results = []

    def send_result(at):
        value, result = ((outv, blocks_out), (gin, grads_out))[at]
        here, there = pl.ds(sec * half, half), pl.ds(other * half, half)
        local = pltpu.make_async_copy(value.at[sec], result.at[0, here], out_send.at[0, at])
        sems = out_send.at[1, at], out_recv.at[at]
        away = remote(value.at[other], result.at[0, here], *sems, other_core)
        local.start()
        away.start()
        results.append((local, away, remote(value.at[other], result.at[0, there], *sems, other_core)))

    wait_pair(0, (0, 1), (0, 1, 2))
    forward_in(0)
    build_masks()
    loads[5].wait()
    bias_sum(1)
    loads[3].wait()
    wait_pair(0, (2,), (4,))
    forward_out(0)
    wait_pair(1, (0, 1), (0, 1, 2))
    forward_in(1)
    wait_pair(1, (2,), (4,))
    last_grad(1)
    loads[4].wait()
    forward_out(1)
    if plan.pool_rows > plan.used_rows:
        pool[plan.used_rows : plan.pool_rows, :] = jnp.zeros(
            (plan.pool_rows - plan.used_rows, 128), BF16
        )
    run((
        (backward_out, 1), (up_weight_grad, 1), 0, (kernel_grad, 1, 2), (kernel_grad, 1, 0),
        (kernel_grad, 1, 1), 0, 1, (backward_mid, 1), 1, (down_weight_grad, 1), 0, 2,
        (backward_in, 1), 2, (up_weight_grad, 0), (backward_out, 0), 1, (kernel_grad, 0, 2), 0,
        (kernel_grad, 0, 0), 4, (kernel_grad, 0, 1), 2, 5, (kernel_grad, 0, 4), 3, 4, 1,
        (kernel_grad, 0, 3), 6, 3, 5, 2, 6, 0, (backward_mid, 0), 1, 4, 5, (down_weight_grad, 0),
        (send_result, 0), (backward_in, 0), (send_result, 1), VECTORS, 8, 7, 3, 2, 6, 0, 7, 4, 8, 5,
        1, 0, 6, 7, 2, 4, 3, 1, 5, 0, 7, VECTORS, 8, 2, 4, 6, 8, 3, 5, 4, 7, 6, 5, 8, VECTORS, 3, 4,
        1, 2, 7, 4, 6, 8, 5, 2, VECTORS, 3, 7, 8, 0, 6, 3, 6, 1, 7, 3, 5, 8, 7, 8,
    ))

    while any(events is not None for events in running.values()):
        run(tuple(range(len(plan.chunks))) + (VECTORS,))
    vec_out[...] = vtotal[len(plan.vec_stages) - 1]
    for local, away, arrives in results:
        local.wait()
        away.wait_send()
        arrives.wait_recv()
    pltpu.make_async_copy(summed, pool_out, out_sem.at[0]).wait()
    for copy in later_sends:
        copy.wait_send()
    for at in range(2):
        everything = summed.at[pl.ds(0, plan.sent_rows)]
        remote(everything, everything, pool_send.at[at], rs_recv.at[0], other_core).wait_send()
    remote(vrecv, vrecv, vec_send.at[0], vec_recv.at[0], other_core).wait_send()


def final_kernel(plan, blocks_in, grads_in, pool_in, vec_in, *refs):
    (
        blocks_out, grads_out, g_in_gain, g_in_shift, g_down, g_down_bias, g_mid_gain, g_mid_shift,
        g_enc, g_dec, g_conv_bias, g_out_gain, g_out_shift, g_up, g_up_bias,
        vec, wide_out, narrow_out, bounce, up_pool, down_pool, tap_pool, up_full, down_full, enc_full, dec_full,
        in_sem, out_sem, vec_sem,
    ) = refs
    sec = lax.axis_index("section")
    width, inner = plan.width, plan.inner
    entering = [
        pltpu.make_async_copy(blocks_in, bounce.at[0], in_sem.at[4]),
        pltpu.make_async_copy(grads_in, bounce.at[1], in_sem.at[5]),
    ]
    vec_load = pltpu.make_async_copy(vec_in, vec, vec_sem.at[0])
    vec_load.start()
    passed = [
        pltpu.make_async_copy(bounce.at[0], blocks_out, out_sem.at[0]),
        pltpu.make_async_copy(bounce.at[1], grads_out, out_sem.at[1]),
    ]
    for copy in entering:
        copy.start()

    def load(name, target, size, sem):
        start = jnp.where(sec == 0, plan.at[name, 0], plan.at[name, 1])
        copy = pltpu.make_async_copy(pool_in.at[pl.ds(pl.multiple_of(start, 16), size)], target, in_sem.at[sem])
        copy.start()
        return copy

    up_load = load("up", up_pool, plan.up_rows, 0)
    down_load = load("down", down_pool, plan.down_rows, 1)
    tap_loads = []
    part = inner // 2
    low = part // 128
    lanes = (plan.in_tiles - 1 - low) * 128
    size = plan.tap_part
    first_tile = sec * low
    for block in (0, 1):
        for tap in range(plan.taps[block]):
            start = plan.at["kernel", block] + tap * plan.tap_rows + first_tile * inner
            at = len(tap_loads)
            copy = pltpu.make_async_copy(
                pool_in.at[pl.ds(pl.multiple_of(start, 16), size)], tap_pool.at[at], in_sem.at[6 + at]
            )
            copy.start()
            tap_loads.append(copy)

    vec_load.wait()
    for at, ref in enumerate((g_in_gain, g_in_shift, g_up_bias)):
        pieces = [vec[2 * at : 2 * at + 1, :], vec[2 * at + 1 : 2 * at + 2, : width - 512]]
        wide_out[at] = jnp.concatenate(pieces, axis=1)
        passed.append(pltpu.make_async_copy(wide_out.at[at], ref, vec_sem.at[1 + at]))
        passed[-1].start()
    for at, ref in enumerate((g_down_bias, g_mid_gain, g_mid_shift, g_conv_bias, g_out_gain, g_out_shift)):
        narrow_out[at] = vec[6 + at : 7 + at, :inner]
        passed.append(pltpu.make_async_copy(narrow_out.at[at], ref, vec_sem.at[4 + at]))
        passed[-1].start()

    def rest_of(ref, position, rest, tiles):
        pieces = [ref[position + tile * rest : position + (tile + 1) * rest, :] for tile in range(tiles)]
        return jnp.concatenate(pieces, axis=1).astype(F32)

    def unpack(ref, full, rows, main, rest, tiles):
        for tile in range(main):
            full[:, tile * 128 : (tile + 1) * 128] = ref[tile * rows : (tile + 1) * rows, :].astype(F32)
        left = rest_of(ref, main * rows, rest, tiles)
        full[:, main * 128 :] = left.T[:rows, :]

    for first, second in zip(entering, passed):
        first.wait()
        second.start()
    up_load.wait()
    unpack(up_pool, up_full, inner, plan.up_main, plan.up_rest, plan.in_tiles)
    up_store = pltpu.make_async_copy(up_full, g_up.at[0], out_sem.at[2])
    up_store.start()
    down_load.wait()
    unpack(down_pool, down_full, inner, plan.up_main, plan.up_rest, plan.in_tiles)
    down_store = pltpu.make_async_copy(down_full, g_down.at[0], out_sem.at[3])
    down_store.start()
    taken = lanes + plan.in_rest
    row = lax.broadcasted_iota(jnp.int32, (taken, part), 0)
    column = lax.broadcasted_iota(jnp.int32, (taken, part), 1)
    choose = jnp.where(row == column + sec * (part - low * 128), 1.0, 0.0).astype(BF16)
    stores = []
    for block, full, target in ((0, enc_full, g_enc), (1, dec_full, g_dec)):
        for tap in range(plan.taps[block]):
            at = tap + block * plan.taps[0]
            tap_loads[at].wait()
            main = jnp.concatenate(
                [tap_pool[at, tile * inner : (tile + 1) * inner, :] for tile in range(lanes // 128)], axis=1
            )
            rest = rest_of(tap_pool.at[at], lanes // 128 * inner, plan.in_rest, plan.in_tiles)
            rest = rest[:, :inner].astype(BF16)
            full[tap] = dot(main, choose[:lanes], 1, 0) + dot(rest, choose[lanes:], 0, 0)
            copy = pltpu.make_async_copy(full.at[tap], target.at[tap], out_sem.at[4 + at])
            copy.start()
            stores.append(copy)
    for copy in passed + [up_store, down_store] + stores:
        copy.wait()


def per_device(plan, *args):
    (
        block_inputs, cotangent, segment_ids, in_gain, in_shift, down_weight, down_bias, mid_gain,
        mid_shift, enc_kernel, dec_kernel, conv_bias, out_gain, out_shift, up_weight, up_bias,
    ) = args
    args = args[:5] + (jnp.swapaxes(down_weight, 1, 2),) + args[6:]
    length, width, inner, half, tokens = plan.length, plan.width, plan.inner, plan.half, plan.tokens
    chunks = len(plan.chunks)
    any_spec = pl.BlockSpec(memory_space=pl.ANY)
    vmem_spec = pl.BlockSpec(memory_space=pltpu.VMEM)
    wide = lambda kind: pltpu.VMEM((2, half, length, width), kind)
    narrow = lambda kind: pltpu.VMEM((2, half, length, inner), kind)
    factor = pltpu.VMEM((2, half, length, 128), F32)
    dma = pltpu.SemaphoreType.DMA
    enc_taps, dec_taps = plan.taps
    blocks, grads, pool, vectors = pl.pallas_call(
        functools.partial(main_kernel, plan),
        out_shape=(
            jax.ShapeDtypeStruct(block_inputs.shape, BF16),
            jax.ShapeDtypeStruct(block_inputs.shape, BF16),
            jax.ShapeDtypeStruct((plan.pool_rows, 128), BF16),
            jax.ShapeDtypeStruct((16, 512), F32),
        ),
        in_specs=[any_spec, any_spec, vmem_spec, vmem_spec, vmem_spec, any_spec, vmem_spec, vmem_spec,
                  vmem_spec, any_spec, any_spec, vmem_spec, vmem_spec, vmem_spec, any_spec, vmem_spec],
        out_specs=(any_spec, any_spec, any_spec, vmem_spec),
        scratch_shapes=[
            pltpu.VMEM((2, half, length, width), BF16),
            pltpu.VMEM((1, half, length, width), BF16),
            pltpu.VMEM((2, inner, width), BF16),
            pltpu.VMEM((2, inner, width), BF16),
            pltpu.VMEM((enc_taps, inner, inner), BF16),
            pltpu.VMEM((dec_taps, inner, inner), BF16),
            pltpu.VMEM((2, 16, width), F32),
            pltpu.VMEM((2,) + segment_ids.shape, jnp.int32),
            pltpu.VMEM((len(OFFSETS), half, length, 128), BF16),
            wide(F32), wide(F32), factor,
            narrow(F32), narrow(F32), factor,
            narrow(F32), narrow(F32), factor,
            wide(BF16),
            pltpu.VMEM((2, half, plan.ext, inner), BF16),
            pltpu.VMEM((enc_taps + dec_taps, half, length, inner), BF16),
            narrow(BF16),
            wide(BF16),
            pltpu.VMEM((2, half, plan.ext, inner), BF16),
            narrow(BF16),
            wide(BF16),
            pltpu.VMEM((1, half, length, inner), F32),
            pltpu.VMEM((plan.pool_rows, 128), BF16),
            pltpu.VMEM((plan.pool_rows, 128), BF16),
            pltpu.VMEM((plan.recv_rows, 128), BF16),
            pltpu.VMEM((2, 16, 512), F32),
            pltpu.VMEM((len(plan.vec_stages), 16, 512), F32),
            pltpu.VMEM((plan.vec_copies, 16, 512), F32),
            pltpu.VMEM((2 * half, MARGIN, inner), BF16),
            dma((6,)), dma((5,)), dma((5,)), dma((2,)), dma((2,)), dma((2, 2)), dma((2, 2)),
            dma((2,)), dma((chunks * plan.most_stages,)), dma((chunks * plan.most_stages,)),
            dma((1,)), dma((len(plan.vec_stages),)),
            dma((1,)), dma((2, 2)), dma((2,)),
        ],
        compiler_params=pltpu.CompilerParams(
            collective_id=0, has_side_effects=True, vmem_limit_bytes=VMEM_LIMIT
        ),
        name="blocks_and_sums",
    )(*args)
    vector = lambda size: jax.ShapeDtypeStruct((1, size), F32)
    part = inner // 2
    results = pl.pallas_call(
        functools.partial(final_kernel, plan),
        out_shape=(
            jax.ShapeDtypeStruct(block_inputs.shape, BF16),
            jax.ShapeDtypeStruct(block_inputs.shape, BF16),
            vector(width), vector(width),
            jax.ShapeDtypeStruct((1, inner, width), F32),
            vector(inner), vector(inner), vector(inner),
            jax.ShapeDtypeStruct((enc_taps, inner, part), F32),
            jax.ShapeDtypeStruct((dec_taps, inner, part), F32),
            vector(inner), vector(inner), vector(inner),
            jax.ShapeDtypeStruct((1, inner, width), F32),
            vector(width),
        ),
        in_specs=[any_spec] * 4,
        out_specs=(any_spec,) * 15,
        scratch_shapes=[
            pltpu.VMEM((16, 512), F32),
            pltpu.VMEM((3, 1, width), F32),
            pltpu.VMEM((6, 1, inner), F32),
            pltpu.VMEM((2,) + block_inputs.shape, BF16),
            pltpu.VMEM((plan.up_rows, 128), BF16),
            pltpu.VMEM((plan.down_rows, 128), BF16),
            pltpu.VMEM((enc_taps + dec_taps, plan.tap_part, 128), BF16),
            pltpu.VMEM((inner, width), F32),
            pltpu.VMEM((inner, width), F32),
            pltpu.VMEM((enc_taps, inner, part), F32),
            pltpu.VMEM((dec_taps, inner, part), F32),
            dma((6 + enc_taps + dec_taps,)), dma((4 + enc_taps + dec_taps,)), dma((10,)),
        ],
        compiler_params=pltpu.CompilerParams(vmem_limit_bytes=VMEM_LIMIT),
        name="unpack_sums",
    )(blocks, grads, pool, vectors)
    return results[:4] + (jnp.swapaxes(results[4], 1, 2),) + results[5:]


def solution(mesh):
    def whole(*args):
        rows, length, width = (
            args[0].shape[1] // mesh.shape["dp"], args[0].shape[2] // mesh.shape["seq"], args[0].shape[3]
        )
        inner = args[9].shape[1]
        plan = Plan(mesh, rows, length, width, inner, args[9].shape[0], args[10].shape[0])
        by_section = P("section", None)
        weight = P("section", None, None)
        data = P("section", "dp", "seq", None)
        return jax.shard_map(
            functools.partial(per_device, plan),
            mesh=mesh,
            in_specs=(
                data, P("dp", "seq", None), P("dp", "seq"), by_section, by_section, weight, by_section,
                by_section, by_section, P(), P(), by_section, by_section, by_section, weight, by_section,
            ),
            out_specs=(
                data, data, by_section, by_section, weight, by_section, by_section, by_section,
                P(None, None, "section"), P(None, None, "section"),
                by_section, by_section, by_section, weight, by_section,
            ),
            check_vma=False,
        )(*args)

    return whole
```

```python
import functools

import jax
import jax.numpy as jnp
from jax import lax
from jax.experimental import pallas as pl
from jax.experimental.pallas import tpu as pltpu
from jax.sharding import PartitionSpec as P

DILATION = 16
MARGIN = 2 * DILATION
EPSILON = 1e-05
MESH = pl.DeviceIdType.MESH
BF16 = jnp.bfloat16
F32 = jnp.float32
OFFSETS = (-2 * DILATION, -DILATION, DILATION, 2 * DILATION)
ROOT = 0.7978845608028654
CUBIC = 0.044715 * ROOT
VMEM_LIMIT = 60 * 2**20
VECTORS = -1


def dot(left, right, left_dim, right_dim):
    return lax.dot_general(
        left, right, (((left_dim,), (right_dim,)), ((), ())), preferred_element_type=F32
    )


def across(column, width):
    whole, rest = divmod(width, 128)
    pieces = [column] * whole
    if rest:
        pieces.append(column[:, :rest])
    return jnp.concatenate(pieces, axis=1) if len(pieces) > 1 else pieces[0]


def norm_act(values, gain, shift):
    scale = 1.0 / values.shape[-1]
    centred = values - jnp.sum(values, axis=-1, keepdims=True) * scale
    variance = jnp.sum(centred * centred, axis=-1, keepdims=True) * scale
    factor = lax.rsqrt(variance + EPSILON)
    normed = centred * factor
    pre = normed * gain + shift
    square = pre * pre
    half = 0.5 + 0.5 * jnp.tanh(pre * (ROOT + CUBIC * square))
    act = pre * half
    slope = half + act * (1.0 - half) * (2.0 * ROOT + 6.0 * CUBIC * square)
    return normed, factor, act, slope


def norm_act_back(upstream, slope, normed, factor, gain):
    scale = 1.0 / normed.shape[-1]
    at_pre = upstream * slope
    shift_grad = jnp.sum(at_pre, axis=0, keepdims=True)
    gain_grad = jnp.sum(at_pre * normed, axis=0, keepdims=True)
    scaled = at_pre * gain
    first = jnp.sum(scaled, axis=-1, keepdims=True) * scale
    second = jnp.sum(scaled * normed, axis=-1, keepdims=True) * scale
    return factor * (scaled - first - normed * second), gain_grad, shift_grad


def row_block(rows):
    best = 16
    for size in range(16, 257, 16):
        if rows % size == 0:
            best = size
    return best


PARTS = 40
CHUNKS = ((4, "std"), (11, "std"), (17, "std"), (22, "std"), (24, "std"), (28, "std"), (32, "std"), (35, "std"), (38, "std"), (40, "std"))


class Plan:
    def __init__(self, mesh, rows, length, width, inner, enc_taps, dec_taps):
        self.rows, self.length, self.width, self.inner = rows, length, width, inner
        self.half = rows // 2
        self.tokens = self.half * length
        self.taps = (enc_taps, dec_taps)
        self.n_dp, self.n_seq = mesh.shape["dp"], mesh.shape["seq"]
        self.ext = length + 2 * MARGIN
        self.up_main, self.up_rest = divmod(width, 128)
        self.in_main, self.in_rest = divmod(inner, 128)
        lanes = lambda size: -(-size // 128)
        self.in_tiles, self.width_tiles = lanes(inner), lanes(width)
        self.up_rows = self.up_main * inner + self.up_rest * self.in_tiles
        self.down_rows = self.up_rows
        self.tap_rows = self.in_main * inner + self.in_rest * self.in_tiles
        self.tap_part = self.tap_rows - inner // 2 // 128 * inner
        position = 0
        self.at = {}
        for name, block, size, pieces in (
            ("up", 1, self.up_rows, 1), ("kernel", 1, self.tap_rows, dec_taps), ("down", 1, self.down_rows, 1),
            ("up", 0, self.up_rows, 1), ("kernel", 0, self.tap_rows, enc_taps), ("down", 0, self.down_rows, 1),
        ):
            self.at[name, block] = position
            position += size * pieces
        self.used_rows = position
        section = [("section", (1, 1), 2)]
        bits = self.n_seq.bit_length() - 1
        assert self.n_seq == 1 << bits
        halves = [("seq", (1 << bit, 1 << (bits - 1 - bit)), 2) for bit in range(bits)]
        direct = [("seq", (1, 1), self.n_seq)] if bits else []
        layers, left, stride = [], self.n_dp, 1
        while left > 1:
            radix = 4 if left % 4 == 0 else 2
            assert left % radix == 0
            layers.append(("dp", (stride, stride), radix))
            left, stride = left // radix, stride * radix
        orders = {"std": section + halves + layers, "dp first": section + layers + halves,
                  "direct": section + direct + layers}
        self.vec_stages = orders["direct"]
        unit = 32 * self.n_seq * self.n_dp
        self.pool_rows = -(-self.used_rows // unit) * unit
        nominal = -(-self.used_rows // 512) * 512
        self.chunks, first = [], 0
        for end, order in CHUNKS:
            last = self.pool_rows if end == PARTS else nominal * end // PARTS // unit * unit
            self.chunks.append((first, last, orders[order]))
            first = last
        self.landing, self.recv_rows = [], 0
        for first, last, stages in self.chunks:
            size, places = last - first, []
            for _, _, radix in stages:
                size //= radix
                places.append(self.recv_rows)
                self.recv_rows += size * (radix - 1)
            self.landing.append(places)
        self.sent_rows = self.pool_rows - self.pool_rows // (unit // 16)
        self.most_stages = max(len(stages) for _, _, stages in self.chunks)
        self.vec_copies = sum(radix - 1 for _, _, radix in self.vec_stages)


def main_kernel(plan, *refs):
    (
        blocks_in, cot_in, seg_in, in_gain, in_shift, down_in, down_bias, mid_gain, mid_shift,
        enc_in, dec_in, conv_bias, out_gain, out_shift, up_in, up_bias,
        blocks_out, grads_out, pool_out, vec_out,
        xin, cot, wd, wu, ek, dk, vec, seg_side, masks,
        n1, s1, q1, n2, s2, q2, n3, s3, q3, fa, mid, win, la, outv, cp, hp, gin, dl,
        pool, summed, recv, vsum, vtotal, vrecv, halo_bytes,
        load_sem, pair_send, pair_recv, seg_send, seg_recv, halo_send, halo_recv,
        pool_send, rs_recv, ag_recv, vec_send, vec_recv, out_sem, out_send, out_recv,
    ) = refs
    length, width, inner, half = plan.length, plan.width, plan.inner, plan.half
    kernels = (ek, dk)
    sec = lax.axis_index("section")
    seq = lax.axis_index("seq")
    other = 1 - sec
    other_core = {"section": other}
    right = {"seq": lax.rem(seq + 1, plan.n_seq)}
    left = {"seq": lax.rem(seq + plan.n_seq - 1, plan.n_seq)}
    later_sends = []

    def remote(src, dst, send, recv, device):
        return pltpu.make_async_remote_copy(
            src_ref=src, dst_ref=dst, send_sem=send, recv_sem=recv,
            device_id=device, device_id_type=MESH,
        )

    own_rows = pl.ds(sec * half, half)
    loads = [
        pltpu.make_async_copy(blocks_in.at[0, own_rows], xin.at[sec], load_sem.at[0]),
        pltpu.make_async_copy(down_in.at[0], wd.at[sec], load_sem.at[1]),
        pltpu.make_async_copy(up_in.at[0], wu.at[sec], load_sem.at[2]),
        pltpu.make_async_copy(enc_in, ek, load_sem.at[3]),
        pltpu.make_async_copy(dec_in, dk, load_sem.at[4]),
        pltpu.make_async_copy(cot_in.at[own_rows], cot.at[0], load_sem.at[5]),
    ]
    loads[0].start()
    loads[1].start()
    vec[...] = jnp.zeros_like(vec)
    for at, ref in enumerate((in_gain, in_shift, up_bias)):
        vec[sec, at : at + 1, :] = ref[...]
    for at, ref in enumerate((down_bias, mid_gain, mid_shift, conv_bias, out_gain, out_shift)):
        vec[sec, 3 + at : 4 + at, :inner] = ref[...]

    known = {}

    def place(stage):
        if stage not in known:
            axis, strides, radix = stage
            index = lax.axis_index(axis)
            stride = strides[0] if strides[0] == strides[1] else jnp.where(sec == 0, *strides)
            digit = lax.rem(lax.div(index, stride), radix)
            others = [
                {axis: index + (lax.rem(digit + step, radix) - digit) * stride}
                for step in range(1, radix)
            ]
            known[stage] = digit, others
        return known[stage]

    greeted = [peer for stage in plan.vec_stages for peer in place(stage)[1]]
    barrier = pltpu.get_barrier_semaphore()
    for peer in greeted:
        pl.semaphore_signal(barrier, inc=1, device_id=peer, device_id_type=MESH)
    pl.semaphore_wait(barrier, len(greeted))

    def pair(src, dst, at):
        copy = remote(src, dst, pair_send.at[at], pair_recv.at[at], other_core)
        copy.start()
        return copy

    def pair_rows(at, low, size):
        for row in range(half):
            rows = pl.ds(low, size)
            pair(blocks_in.at[0, other * half + row, rows], xin.at[sec, row, rows], at)

    pair(vec.at[sec], vec.at[sec], 0)
    pair_rows(1, 0, MARGIN)
    pair_rows(1, length - MARGIN, MARGIN)
    pair(down_in.at[0], wd.at[sec], 2)
    pair_rows(3, MARGIN, length - 2 * MARGIN)
    pair(up_in.at[0], wu.at[sec], 4)
    pair_whole = (
        vec.at[other], xin.at[other, :, pl.ds(0, 2 * MARGIN)], wd.at[other],
        xin.at[other, :, pl.ds(0, length - 2 * MARGIN)], wu.at[other],
    )
    arriving = [
        remote(ref, ref, pair_send.at[at], pair_recv.at[at], other_core)
        for at, ref in enumerate(pair_whole)
    ]
    later_sends.extend(arriving)
    seg_copies = [
        remote(seg_in, seg_side.at[0], seg_send.at[0], seg_recv.at[0], right),
        remote(seg_in, seg_side.at[1], seg_send.at[1], seg_recv.at[1], left),
    ]
    for copy in seg_copies:
        copy.start()
    later_sends.extend(seg_copies)
    for load in loads[2:]:
        load.start()
    vsum[...] = jnp.zeros_like(vsum)

    def wait_pair(block, local, away):
        @pl.when(sec == block)
        def _():
            for at in local:
                loads[at].wait()

        @pl.when(sec != block)
        def _():
            for at in away:
                arriving[at].wait_recv()

    def build_masks():
        for copy in seg_copies:
            copy.wait_recv()
        ext = plan.ext
        position = lax.broadcasted_iota(jnp.int32, (ext, length), 0)
        token = lax.broadcasted_iota(jnp.int32, (ext, length), 1)
        for row in range(half):
            at = pl.ds(sec * half + row, 1)
            own = (seg_in[at, :] + 1).astype(F32)
            before = jnp.where(seq > 0, (seg_side[0, at, :] + 1).astype(F32), 0.0)
            after = jnp.where(seq < plan.n_seq - 1, (seg_side[1, at, :] + 1).astype(F32), 0.0)
            numbers = jnp.where(position - MARGIN == token, own, 0.0)
            numbers = numbers + jnp.where(position + (length - MARGIN) == token, before, 0.0)
            numbers = numbers + jnp.where(position - (length + MARGIN) == token, after, 0.0)
            numbers = dot(numbers.astype(BF16), jnp.ones((length, 128), BF16), 1, 0)
            here = numbers[MARGIN : MARGIN + length]
            for at_offset, offset in enumerate(OFFSETS):
                there = numbers[MARGIN + offset : MARGIN + offset + length]
                masks[at_offset, row] = jnp.where(there == here, 1.0, 0.0).astype(BF16)

    edges = [span for row in range(half) for span in ((row, 0, MARGIN), (row, length - MARGIN, length))]
    middle = [(row, MARGIN, length - MARGIN) for row in range(half)]
    everywhere = [(row, 0, length) for row in range(half)]

    def take(ref, at, part, offset=0):
        return jnp.concatenate(
            [ref[at, row, low + offset : high + offset, :] for row, low, high in part], axis=0
        )

    def put(ref, at, part, value, offset=0):
        done = 0
        for row, low, high in part:
            ref[at, row, low + offset : high + offset, :] = value[done : done + high - low]
            done += high - low

    def window(ref, block, offset):
        piece = take(ref, block, everywhere, MARGIN + offset)
        if offset == 0:
            return piece
        return piece * across(take(masks, OFFSETS.index(offset), everywhere), inner)

    def params(block):
        wide = [vec[block, at : at + 1, :] for at in range(3)]
        narrow = [vec[block, 3 + at : 4 + at, :inner] for at in range(6)]
        return wide + narrow

    def halo_start(ref, which, block):
        sems = halo_send.at[which, block], halo_recv.at[which, block]
        for row in range(half):
            if block == 0 or which == 0:
                remote(
                    ref.at[block, row, pl.ds(length, MARGIN)], ref.at[block, row, pl.ds(0, MARGIN)],
                    *sems, right,
                ).start()
            if block == 0 or which == 1:
                remote(
                    ref.at[block, row, pl.ds(MARGIN, MARGIN)],
                    ref.at[block, row, pl.ds(length + MARGIN, MARGIN)], *sems, left,
                ).start()

    def halo_wait(which, block):
        count = half * (2 if block == 0 else 1)
        everything = halo_bytes.at[pl.ds(0, count)]
        remote(
            everything, everything, halo_send.at[which, block], halo_recv.at[which, block], right
        ).wait()

    def entry(block, part):
        values = take(xin, block, part).astype(F32)
        if block == 1:
            values = values + take(outv, 0, part).astype(F32)
        return values

    def spread(factor):
        return jnp.broadcast_to(factor, (factor.shape[0], 128))

    def forward_in(block):
        p = params(block)
        for part in (edges, middle):
            if part is middle:
                wait_pair(block, (), (3,))
            normed, factor, act, slope = norm_act(entry(block, part), p[0], p[1])
            put(n1, block, part, normed)
            put(s1, block, part, slope)
            put(q1, block, part, spread(factor))
            act = act.astype(BF16)
            put(fa, block, part, act)
            hidden = dot(act, wd[block], 1, 1) + p[3]
            normed, factor, act, slope = norm_act(hidden, p[4], p[5])
            put(n2, block, part, normed)
            put(s2, block, part, slope)
            put(q2, block, part, spread(factor))
            put(mid, block, part, act.astype(BF16), MARGIN)
            if part is edges:
                halo_start(mid, 0, block)

    def forward_out(block):
        p = params(block)
        halo_wait(0, block)
        total = None
        for tap in range(plan.taps[block]):
            piece = window(mid, block, (tap - 2) * DILATION)
            put(win, block * plan.taps[0] + tap, everywhere, piece)
            term = dot(piece, kernels[block][tap], 1, 0)
            total = term if total is None else total + term
        normed, factor, act, slope = norm_act(total + p[6], p[7], p[8])
        put(n3, block, everywhere, normed)
        put(s3, block, everywhere, slope)
        put(q3, block, everywhere, spread(factor))
        act = act.astype(BF16)
        put(la, block, everywhere, act)
        result = entry(block, everywhere) + dot(act, wu[block], 1, 0) + p[2]
        put(outv, block, everywhere, result.astype(BF16))

    def add_wide(block, at, value):
        vsum[block, at : at + 1, :] += value[:, :512]
        vsum[block, at + 1 : at + 2, : width - 512] += value[:, 512:]

    def add_narrow(block, at, value):
        vsum[block, at : at + 1, :inner] += value

    def upstream_of(block, part):
        return take(cot, 0, part) if block == 1 else take(gin, 1, part)

    def last_grad(block):
        put(dl, 0, everywhere, dot(upstream_of(block, everywhere), wu[block], 1, 1))

    def bias_sum(block):
        incoming = upstream_of(block, everywhere).astype(F32)
        add_wide(block, 4, jnp.sum(incoming, axis=0, keepdims=True))

    def backward_out(block):
        p = params(block)
        for part in (edges, middle):
            if block == 1:
                d_last = take(dl, 0, part)
            else:
                incoming = upstream_of(block, part)
                add_wide(block, 4, jnp.sum(incoming.astype(F32), axis=0, keepdims=True))
                d_last = dot(incoming, wu[block], 1, 1)
            d_conv, gain_grad, shift_grad = norm_act_back(
                d_last, take(s3, block, part), take(n3, block, part),
                across(take(q3, block, part), inner), p[7],
            )
            add_narrow(block, 10, gain_grad)
            add_narrow(block, 11, shift_grad)
            add_narrow(block, 9, jnp.sum(d_conv, axis=0, keepdims=True))
            put(cp, block, part, d_conv.astype(BF16), MARGIN)
            if part is edges:
                halo_start(cp, 1, block)

    def backward_mid(block):
        p = params(block)
        halo_wait(1, block)
        total = None
        for tap in range(plan.taps[block]):
            term = dot(window(cp, block, -(tap - 2) * DILATION), kernels[block][tap], 1, 1)
            total = term if total is None else total + term
        d_hidden, gain_grad, shift_grad = norm_act_back(
            total, take(s2, block, everywhere), take(n2, block, everywhere),
            across(take(q2, block, everywhere), inner), p[4],
        )
        add_narrow(block, 7, gain_grad)
        add_narrow(block, 8, shift_grad)
        add_narrow(block, 6, jnp.sum(d_hidden, axis=0, keepdims=True))
        put(hp, block, everywhere, d_hidden.astype(BF16))

    def backward_in(block):
        p = params(block)
        d_first = dot(take(hp, block, everywhere), wd[block], 1, 0)
        d_entry, gain_grad, shift_grad = norm_act_back(
            d_first, take(s1, block, everywhere), take(n1, block, everywhere),
            across(take(q1, block, everywhere), width), p[0],
        )
        add_wide(block, 0, gain_grad)
        add_wide(block, 2, shift_grad)
        incoming = upstream_of(block, everywhere).astype(F32)
        put(gin, block, everywhere, (incoming + d_entry).astype(BF16))

    def to_pool(position, left_value, right_value):
        rows, columns = left_value.shape[1], right_value.shape[1]
        main, rest = divmod(columns, 128)
        product = dot(left_value, right_value[:, : main * 128], 0, 0).astype(BF16)
        for tile in range(main):
            pool[position + tile * rows : position + (tile + 1) * rows, :] = product[
                :, tile * 128 : (tile + 1) * 128
            ]
        position += main * rows
        product = dot(right_value[:, main * 128 :], left_value, 0, 0).astype(BF16)
        for tile in range(-(-rows // 128)):
            lanes = min(128, rows - tile * 128)
            pool[position + tile * rest : position + (tile + 1) * rest, :lanes] = product[
                :, tile * 128 : tile * 128 + lanes
            ]

    def up_weight_grad(block):
        to_pool(plan.at["up", block], take(la, block, everywhere), upstream_of(block, everywhere))

    def kernel_grad(block, tap):
        to_pool(
            plan.at["kernel", block] + tap * plan.tap_rows,
            take(win, block * plan.taps[0] + tap, everywhere), take(cp, block, everywhere, MARGIN),
        )

    def down_weight_grad(block):
        to_pool(plan.at["down", block], take(hp, block, everywhere), take(fa, block, everywhere))

    running = {}

    def sum_chunk(chunk):
        first, last, stages = plan.chunks[chunk]
        places = [place(stage) for stage in stages]
        sizes, offsets = [last - first], [first]
        for (digit, _), (_, _, radix) in zip(places, stages):
            sizes.append(sizes[-1] // radix)
            offsets.append(pl.multiple_of(offsets[-1] + digit * sizes[-1], 16))

        def part(ref, stage, digit):
            size = sizes[stage + 1]
            return ref.at[pl.ds(pl.multiple_of(offsets[stage] + digit * size, 16), size)]

        for stage, (_, _, radix) in enumerate(stages):
            digit, others = places[stage]
            size, landing = sizes[stage + 1], plan.landing[chunk][stage]
            sem = rs_recv.at[chunk * plan.most_stages + stage]
            for step in range(1, radix):
                remote(
                    part(pool, stage, lax.rem(digit + step, radix)),
                    recv.at[pl.ds(landing + (step - 1) * size, size)],
                    pool_send.at[0], sem, others[step - 1],
                ).start()
            yield
            landed = recv.at[pl.ds(landing, (radix - 1) * size)]
            remote(landed, landed, pool_send.at[0], sem, others[0]).wait_recv()
            target = summed if stage + 1 == len(stages) else pool
            block = row_block(size)

            def add(at, carry):
                own = pl.ds(pl.multiple_of(offsets[stage + 1] + at * block, 16), block)
                total = pool[own, :].astype(F32)
                for step in range(radix - 1):
                    from_row = pl.multiple_of(landing + step * size + at * block, 16)
                    total = total + recv[pl.ds(from_row, block), :].astype(F32)
                target[own, :] = total.astype(BF16)
                return carry

            lax.fori_loop(0, size // block, add, 0)
        for stage in reversed(range(len(stages))):
            radix = stages[stage][2]
            digit, others = places[stage]
            size = sizes[stage + 1]
            sem = ag_recv.at[chunk * plan.most_stages + stage]
            own = part(summed, stage, digit)
            for step in range(1, radix):
                remote(own, own, pool_send.at[1], sem, others[step - 1]).start()
            yield
            arriving = summed.at[pl.ds(first, (radix - 1) * size)]
            remote(arriving, arriving, pool_send.at[1], sem, others[0]).wait_recv()
        whole = pl.ds(first, last - first)
        pltpu.make_async_copy(summed.at[whole], pool_out.at[whole], out_sem.at[0]).start()

    def sum_vectors():
        total, slot = None, 0
        for at, stage in enumerate(plan.vec_stages):
            digit, others = place(stage)
            count = stage[2] - 1
            for step in range(count):
                source = vsum.at[other] if at == 0 else vtotal.at[at - 1]
                remote(
                    source, vrecv.at[slot + step], vec_send.at[0], vec_recv.at[at], others[step]
                ).start()
            yield
            landed = vrecv.at[pl.ds(slot, count)]
            remote(landed, landed, vec_send.at[0], vec_recv.at[at], others[0]).wait_recv()
            total = vsum[sec] if at == 0 else vtotal[at - 1]
            for step in range(count):
                total = total + vrecv[slot + step]
            vtotal[at] = total
            slot += count

    def tick(which):
        if which not in running:
            running[which] = sum_vectors() if which == VECTORS else sum_chunk(which)
        if running[which] is not None and next(running[which], "done") == "done":
            running[which] = None

    def run(steps):
        for step in steps:
            if isinstance(step, int):
                if step == VECTORS or plan.chunks[step][0] < plan.chunks[step][1]:
                    tick(step)
            else:
                step[0](*step[1:])

    results = []

    def send_result(at):
        value, result = ((outv, blocks_out), (gin, grads_out))[at]
        here, there = pl.ds(sec * half, half), pl.ds(other * half, half)
        local = pltpu.make_async_copy(value.at[sec], result.at[0, here], out_send.at[0, at])
        sems = out_send.at[1, at], out_recv.at[at]
        away = remote(value.at[other], result.at[0, here], *sems, other_core)
        local.start()
        away.start()
        results.append((local, away, remote(value.at[other], result.at[0, there], *sems, other_core)))

    wait_pair(0, (0, 1), (0, 1, 2))
    forward_in(0)
    build_masks()
    loads[5].wait()
    bias_sum(1)
    loads[3].wait()
    wait_pair(0, (2,), (4,))
    forward_out(0)
    wait_pair(1, (0, 1), (0, 1, 2))
    forward_in(1)
    wait_pair(1, (2,), (4,))
    last_grad(1)
    loads[4].wait()
    forward_out(1)
    if plan.pool_rows > plan.used_rows:
        pool[plan.used_rows : plan.pool_rows, :] = jnp.zeros(
            (plan.pool_rows - plan.used_rows, 128), BF16
        )
    run((
        (up_weight_grad, 1), 0, (backward_out, 1), (kernel_grad, 1, 0), (kernel_grad, 1, 2),
        (kernel_grad, 1, 1), 0, 1, (backward_mid, 1), 1, (down_weight_grad, 1), 2, (backward_in, 1),
        0, 2, (backward_out, 0), (up_weight_grad, 0), 1, 3, (kernel_grad, 0, 0),
        (kernel_grad, 0, 2), 0, (kernel_grad, 0, 1), 4, 3, 5, 2, (kernel_grad, 0, 3), 4, 1, 6, 5,
        (backward_mid, 0), (send_result, 0), 0, 2, 3, (kernel_grad, 0, 4), 6, (down_weight_grad, 0),
        8, 9, 5, 1, 7, 4, 8, 3, 9, 7, 0, (backward_in, 0), (send_result, 1), 2, 6, VECTORS, 8,
        VECTORS, 5, 4, 1, 3, 7, 9, 0, 8, 6, 2, 1, 4, 5, 3, 7, 9, 8, 2, 6, 4, 5, 3, 7, 9, 8, 4,
        VECTORS, 6, 0, 5, 7, 2, 9, 0, 8, 1, 6, 7, 9, VECTORS, 2, 5, 3, 8, 5, 4, 8, 1, 6, 7, 4, 9, 6,
        3, 7, 9,
    ))

    while any(events is not None for events in running.values()):
        run(tuple(range(len(plan.chunks))) + (VECTORS,))
    vec_out[...] = vtotal[len(plan.vec_stages) - 1]
    for local, away, arrives in results:
        local.wait()
        away.wait_send()
        arrives.wait_recv()
    pltpu.make_async_copy(summed, pool_out, out_sem.at[0]).wait()
    for copy in later_sends:
        copy.wait_send()
    for at in range(2):
        everything = summed.at[pl.ds(0, plan.sent_rows)]
        remote(everything, everything, pool_send.at[at], rs_recv.at[0], other_core).wait_send()
    remote(vrecv, vrecv, vec_send.at[0], vec_recv.at[0], other_core).wait_send()


def final_kernel(plan, blocks_in, grads_in, pool_in, vec_in, *refs):
    (
        blocks_out, grads_out, g_in_gain, g_in_shift, g_down, g_down_bias, g_mid_gain, g_mid_shift,
        g_enc, g_dec, g_conv_bias, g_out_gain, g_out_shift, g_up, g_up_bias,
        vec, wide_out, narrow_out, bounce, up_pool, down_pool, tap_pool, up_full, down_full, enc_full, dec_full,
        in_sem, out_sem, vec_sem,
    ) = refs
    sec = lax.axis_index("section")
    width, inner = plan.width, plan.inner
    entering = [
        pltpu.make_async_copy(blocks_in, bounce.at[0], in_sem.at[4]),
        pltpu.make_async_copy(grads_in, bounce.at[1], in_sem.at[5]),
    ]
    vec_load = pltpu.make_async_copy(vec_in, vec, vec_sem.at[0])
    vec_load.start()
    passed = [
        pltpu.make_async_copy(bounce.at[0], blocks_out, out_sem.at[0]),
        pltpu.make_async_copy(bounce.at[1], grads_out, out_sem.at[1]),
    ]
    for copy in entering:
        copy.start()

    def load(name, target, size, sem):
        start = jnp.where(sec == 0, plan.at[name, 0], plan.at[name, 1])
        copy = pltpu.make_async_copy(pool_in.at[pl.ds(pl.multiple_of(start, 16), size)], target, in_sem.at[sem])
        copy.start()
        return copy

    up_load = load("up", up_pool, plan.up_rows, 0)
    down_load = load("down", down_pool, plan.down_rows, 1)
    tap_loads = []
    part = inner // 2
    low = part // 128
    lanes = (plan.in_tiles - 1 - low) * 128
    size = plan.tap_part
    first_tile = sec * low
    for block in (0, 1):
        for tap in range(plan.taps[block]):
            start = plan.at["kernel", block] + tap * plan.tap_rows + first_tile * inner
            at = len(tap_loads)
            copy = pltpu.make_async_copy(
                pool_in.at[pl.ds(pl.multiple_of(start, 16), size)], tap_pool.at[at], in_sem.at[6 + at]
            )
            copy.start()
            tap_loads.append(copy)

    vec_load.wait()
    for at, ref in enumerate((g_in_gain, g_in_shift, g_up_bias)):
        pieces = [vec[2 * at : 2 * at + 1, :], vec[2 * at + 1 : 2 * at + 2, : width - 512]]
        wide_out[at] = jnp.concatenate(pieces, axis=1)
        passed.append(pltpu.make_async_copy(wide_out.at[at], ref, vec_sem.at[1 + at]))
        passed[-1].start()
    for at, ref in enumerate((g_down_bias, g_mid_gain, g_mid_shift, g_conv_bias, g_out_gain, g_out_shift)):
        narrow_out[at] = vec[6 + at : 7 + at, :inner]
        passed.append(pltpu.make_async_copy(narrow_out.at[at], ref, vec_sem.at[4 + at]))
        passed[-1].start()

    def rest_of(ref, position, rest, tiles):
        pieces = [ref[position + tile * rest : position + (tile + 1) * rest, :] for tile in range(tiles)]
        return jnp.concatenate(pieces, axis=1).astype(F32)

    def unpack(ref, full, rows, main, rest, tiles):
        for tile in range(main):
            full[:, tile * 128 : (tile + 1) * 128] = ref[tile * rows : (tile + 1) * rows, :].astype(F32)
        left = rest_of(ref, main * rows, rest, tiles)
        full[:, main * 128 :] = left.T[:rows, :]

    for first, second in zip(entering, passed):
        first.wait()
        second.start()
    up_load.wait()
    unpack(up_pool, up_full, inner, plan.up_main, plan.up_rest, plan.in_tiles)
    up_store = pltpu.make_async_copy(up_full, g_up.at[0], out_sem.at[2])
    up_store.start()
    down_load.wait()
    unpack(down_pool, down_full, inner, plan.up_main, plan.up_rest, plan.in_tiles)
    down_store = pltpu.make_async_copy(down_full, g_down.at[0], out_sem.at[3])
    down_store.start()
    taken = lanes + plan.in_rest
    row = lax.broadcasted_iota(jnp.int32, (taken, part), 0)
    column = lax.broadcasted_iota(jnp.int32, (taken, part), 1)
    choose = jnp.where(row == column + sec * (part - low * 128), 1.0, 0.0).astype(BF16)
    stores = []
    for block, full, target in ((0, enc_full, g_enc), (1, dec_full, g_dec)):
        for tap in range(plan.taps[block]):
            at = tap + block * plan.taps[0]
            tap_loads[at].wait()
            main = jnp.concatenate(
                [tap_pool[at, tile * inner : (tile + 1) * inner, :] for tile in range(lanes // 128)], axis=1
            )
            rest = rest_of(tap_pool.at[at], lanes // 128 * inner, plan.in_rest, plan.in_tiles)
            rest = rest[:, :inner].astype(BF16)
            full[tap] = dot(main, choose[:lanes], 1, 0) + dot(rest, choose[lanes:], 0, 0)
            copy = pltpu.make_async_copy(full.at[tap], target.at[tap], out_sem.at[4 + at])
            copy.start()
            stores.append(copy)
    for copy in passed + [up_store, down_store] + stores:
        copy.wait()


def per_device(plan, *args):
    (
        block_inputs, cotangent, segment_ids, in_gain, in_shift, down_weight, down_bias, mid_gain,
        mid_shift, enc_kernel, dec_kernel, conv_bias, out_gain, out_shift, up_weight, up_bias,
    ) = args
    args = args[:5] + (jnp.swapaxes(down_weight, 1, 2),) + args[6:]
    length, width, inner, half, tokens = plan.length, plan.width, plan.inner, plan.half, plan.tokens
    chunks = len(plan.chunks)
    any_spec = pl.BlockSpec(memory_space=pl.ANY)
    vmem_spec = pl.BlockSpec(memory_space=pltpu.VMEM)
    wide = lambda kind: pltpu.VMEM((2, half, length, width), kind)
    narrow = lambda kind: pltpu.VMEM((2, half, length, inner), kind)
    factor = pltpu.VMEM((2, half, length, 128), F32)
    dma = pltpu.SemaphoreType.DMA
    enc_taps, dec_taps = plan.taps
    blocks, grads, pool, vectors = pl.pallas_call(
        functools.partial(main_kernel, plan),
        out_shape=(
            jax.ShapeDtypeStruct(block_inputs.shape, BF16),
            jax.ShapeDtypeStruct(block_inputs.shape, BF16),
            jax.ShapeDtypeStruct((plan.pool_rows, 128), BF16),
            jax.ShapeDtypeStruct((16, 512), F32),
        ),
        in_specs=[any_spec, any_spec, vmem_spec, vmem_spec, vmem_spec, any_spec, vmem_spec, vmem_spec,
                  vmem_spec, any_spec, any_spec, vmem_spec, vmem_spec, vmem_spec, any_spec, vmem_spec],
        out_specs=(any_spec, any_spec, any_spec, vmem_spec),
        scratch_shapes=[
            pltpu.VMEM((2, half, length, width), BF16),
            pltpu.VMEM((1, half, length, width), BF16),
            pltpu.VMEM((2, inner, width), BF16),
            pltpu.VMEM((2, inner, width), BF16),
            pltpu.VMEM((enc_taps, inner, inner), BF16),
            pltpu.VMEM((dec_taps, inner, inner), BF16),
            pltpu.VMEM((2, 16, width), F32),
            pltpu.VMEM((2,) + segment_ids.shape, jnp.int32),
            pltpu.VMEM((len(OFFSETS), half, length, 128), BF16),
            wide(F32), wide(F32), factor,
            narrow(F32), narrow(F32), factor,
            narrow(F32), narrow(F32), factor,
            wide(BF16),
            pltpu.VMEM((2, half, plan.ext, inner), BF16),
            pltpu.VMEM((enc_taps + dec_taps, half, length, inner), BF16),
            narrow(BF16),
            wide(BF16),
            pltpu.VMEM((2, half, plan.ext, inner), BF16),
            narrow(BF16),
            wide(BF16),
            pltpu.VMEM((1, half, length, inner), F32),
            pltpu.VMEM((plan.pool_rows, 128), BF16),
            pltpu.VMEM((plan.pool_rows, 128), BF16),
            pltpu.VMEM((plan.recv_rows, 128), BF16),
            pltpu.VMEM((2, 16, 512), F32),
            pltpu.VMEM((len(plan.vec_stages), 16, 512), F32),
            pltpu.VMEM((plan.vec_copies, 16, 512), F32),
            pltpu.VMEM((2 * half, MARGIN, inner), BF16),
            dma((6,)), dma((5,)), dma((5,)), dma((2,)), dma((2,)), dma((2, 2)), dma((2, 2)),
            dma((2,)), dma((chunks * plan.most_stages,)), dma((chunks * plan.most_stages,)),
            dma((1,)), dma((len(plan.vec_stages),)),
            dma((1,)), dma((2, 2)), dma((2,)),
        ],
        compiler_params=pltpu.CompilerParams(
            collective_id=0, has_side_effects=True, vmem_limit_bytes=VMEM_LIMIT
        ),
        name="blocks_and_sums",
    )(*args)
    vector = lambda size: jax.ShapeDtypeStruct((1, size), F32)
    part = inner // 2
    results = pl.pallas_call(
        functools.partial(final_kernel, plan),
        out_shape=(
            jax.ShapeDtypeStruct(block_inputs.shape, BF16),
            jax.ShapeDtypeStruct(block_inputs.shape, BF16),
            vector(width), vector(width),
            jax.ShapeDtypeStruct((1, inner, width), F32),
            vector(inner), vector(inner), vector(inner),
            jax.ShapeDtypeStruct((enc_taps, inner, part), F32),
            jax.ShapeDtypeStruct((dec_taps, inner, part), F32),
            vector(inner), vector(inner), vector(inner),
            jax.ShapeDtypeStruct((1, inner, width), F32),
            vector(width),
        ),
        in_specs=[any_spec] * 4,
        out_specs=(any_spec,) * 15,
        scratch_shapes=[
            pltpu.VMEM((16, 512), F32),
            pltpu.VMEM((3, 1, width), F32),
            pltpu.VMEM((6, 1, inner), F32),
            pltpu.VMEM((2,) + block_inputs.shape, BF16),
            pltpu.VMEM((plan.up_rows, 128), BF16),
            pltpu.VMEM((plan.down_rows, 128), BF16),
            pltpu.VMEM((enc_taps + dec_taps, plan.tap_part, 128), BF16),
            pltpu.VMEM((inner, width), F32),
            pltpu.VMEM((inner, width), F32),
            pltpu.VMEM((enc_taps, inner, part), F32),
            pltpu.VMEM((dec_taps, inner, part), F32),
            dma((6 + enc_taps + dec_taps,)), dma((4 + enc_taps + dec_taps,)), dma((10,)),
        ],
        compiler_params=pltpu.CompilerParams(vmem_limit_bytes=VMEM_LIMIT),
        name="unpack_sums",
    )(blocks, grads, pool, vectors)
    return results[:4] + (jnp.swapaxes(results[4], 1, 2),) + results[5:]


def solution(mesh):
    def whole(*args):
        rows, length, width = (
            args[0].shape[1] // mesh.shape["dp"], args[0].shape[2] // mesh.shape["seq"], args[0].shape[3]
        )
        inner = args[9].shape[1]
        plan = Plan(mesh, rows, length, width, inner, args[9].shape[0], args[10].shape[0])
        by_section = P("section", None)
        weight = P("section", None, None)
        data = P("section", "dp", "seq", None)
        return jax.shard_map(
            functools.partial(per_device, plan),
            mesh=mesh,
            in_specs=(
                data, P("dp", "seq", None), P("dp", "seq"), by_section, by_section, weight, by_section,
                by_section, by_section, P(), P(), by_section, by_section, by_section, weight, by_section,
            ),
            out_specs=(
                data, data, by_section, by_section, weight, by_section, by_section, by_section,
                P(None, None, "section"), P(None, None, "section"),
                by_section, by_section, by_section, weight, by_section,
            ),
            check_vma=False,
        )(*args)

    return whole
```
